32 devices in a mesh: layer: 4 (over z), row: 8 (over y, x, core).
Axes of the slice: x: 2, y: 2, z: 4, core: 2. Of those that a mesh axis runs over, the one named last changes fastest.
Arguments:
- tile_left: bfloat16 [48, 4, 64, 1024], P('row', 'layer'), may hold values from -6 to 6
- tile_right: bfloat16 [48, 4, 64, 1024], P('row', 'layer'), may hold values from -0.1875 to 0.1875
- tile_mask: int32 [48, 4], P('row', 'layer'), may hold values from 0 to 1, as said below
- orig_left: bfloat16 [48, 64, 1024], P('row'), may hold values from -6 to 6
- orig_right: bfloat16 [48, 64, 1024], P('row'), may hold values from -0.75 to 0.75
- pivot_left: bfloat16 [4, 64, 1024], P('layer', None, 'row'), may hold values from -6 to 6
- pivot_right: bfloat16 [4, 64, 1024], P('layer', None, 'row'), may hold values from -0.1875 to 0.1875
- sketch: bfloat16 [64, 1024], replicated, may hold values from -0.1875 to 0.1875
- pivot_factor: float32 [1024, 1024], P(('layer', 'row')), as said below
Outputs:
- solved_factor: float32 [48, 64, 1024], P('row')
The draws below stay inside these ranges and needn't reach their ends.
Inputs may be any that keep to these rules, and one draw needn't show every extreme that they name: `tile_mask`: every tile row is updated by at least one earlier panel. `pivot_factor`: lower triangular with a positive diagonal.
All inputs are finite; a program needn't handle non-finite values.
Results may differ from the reference program's by a relative error of at most 0.0003.
Values may be sent and summed in bfloat16 or wider, within the bound.
A program may use at most 64 MiB of HBM per device.

```python
import jax
import jax.numpy as jnp
from jax import lax

B = 1024
R = 64
NT = 48
K = 4


def draw_tile_mask(key, part):
    first_key, second_key = jax.random.split(jax.random.fold_in(key, 23))
    random_bits = jax.random.randint(first_key, (NT, K), 0, 2, dtype=jnp.int32)
    forced = jax.random.randint(second_key, (NT, 1), 0, K, dtype=jnp.int32)
    panels = lax.broadcasted_iota(jnp.int32, (NT, K), 1)
    return jnp.maximum(random_bits, (panels == forced).astype(jnp.int32))


def draw_pivot_factor(key, part):
    first_key, second_key = jax.random.split(jax.random.fold_in(key, 11))
    row_index = lax.broadcasted_iota(jnp.int32, (B, B), 0)
    col_index = lax.broadcasted_iota(jnp.int32, (B, B), 1)
    noise = jax.random.normal(first_key, (B, B), jnp.float32) * (0.5 * B ** (-0.5))
    diagonal = jax.random.uniform(second_key, (B, 1), jnp.float32, 1.5, 2.5)
    lower_part = jnp.where(row_index > col_index, noise, 0.0)
    return lower_part + jnp.where(row_index == col_index, diagonal, 0.0)


def levels(rng, shape, shards, smallest, high):
    gain = 1.0
    for axis_at, blocks in shards:
        draws = jax.random.uniform(jax.random.fold_in(jax.random.fold_in(rng, 6), axis_at), (blocks,), jnp.float32, smallest / len(shards), high / len(shards))
        gain = gain * jnp.repeat(jnp.exp(draws), shape[axis_at] // blocks).reshape((-1,) + (1,) * (len(shape) - 1 - axis_at))
    return gain


def centred(key, extent, width, most, cuts=(), kind=jnp.bfloat16):
    gain = levels(key, extent, cuts, -0.22, 0.18) if cuts else 1.0
    values = jax.random.normal(key, extent, jnp.float32) * width * gain
    return jnp.minimum(jnp.maximum(values, -most), most).astype(kind)


def setup_inputs(seed: int = 0) -> dict:
    seeds = jax.random.split(jax.random.key(seed), 10)
    tile_left = centred(seeds[0], (NT, K, R, B), 1.0, 6.0, ((0, 8), (1, 4)))
    tile_right = centred(seeds[1], (NT, K, R, B), B ** -0.5, 0.1875, ((0, 8), (1, 4)))
    tile_mask = draw_tile_mask(jax.random.fold_in(seeds[9], 71), 0)
    orig_left = centred(seeds[3], (NT, R, B), 1.0, 6.0, ((0, 8),))
    orig_right = centred(seeds[4], (NT, R, B), R ** -0.5, 0.75, ((0, 8),))
    pivot_left = centred(seeds[5], (K, R, B), (B ** 0.5 / R), 6.0, ((0, 4), (2, 8)))
    pivot_right = centred(seeds[6], (K, R, B), B ** -0.5, 0.1875, ((0, 4), (2, 8)))
    sketch = centred(seeds[7], (R, B), B ** -0.5, 0.1875)
    pivot_factor = draw_pivot_factor(jax.random.fold_in(seeds[9], 71), 0)
    return dict(tile_left=tile_left, tile_right=tile_right, tile_mask=tile_mask, orig_left=orig_left, orig_right=orig_right, pivot_left=pivot_left, pivot_right=pivot_right, sketch=sketch, pivot_factor=pivot_factor)


def reference(tile_left, tile_right, tile_mask, orig_left, orig_right, pivot_left, pivot_right, sketch, pivot_factor):
    highest = lax.Precision.HIGHEST
    sketched = jnp.einsum('kqb,sb->kqs', pivot_left.astype(jnp.float32), sketch.astype(jnp.float32), preferred_element_type=jnp.float32)
    pivot_float = pivot_left.astype(jnp.float32)

    def one_tile(items):
        left_tile, right_tile, mask_row, left_orig, right_orig = items
        coupling = jnp.einsum('kqb,ksb->kqs', right_tile.astype(jnp.float32), pivot_right.astype(jnp.float32), preferred_element_type=jnp.float32)
        weights = mask_row.astype(jnp.float32)[:, None, None]
        update_left = jnp.einsum('kqs,kqb->ksb', coupling, left_tile.astype(jnp.float32), precision=highest) * weights
        orig_float = left_orig.astype(jnp.float32)
        orig_sketch = jnp.einsum('qb,sb->qs', right_orig.astype(jnp.float32), sketch.astype(jnp.float32), preferred_element_type=jnp.float32)
        sample = jnp.einsum('qb,qs->sb', orig_float, orig_sketch, precision=highest) - jnp.einsum('kqb,kqs->sb', update_left, sketched, precision=highest)
        gram_matrix = jnp.einsum('qb,sb->qs', sample, sample, precision=highest)
        factor = jnp.linalg.cholesky(gram_matrix)
        row_basis = jax.scipy.linalg.solve_triangular(factor, sample, lower=True)
        projected = jnp.einsum('kqb,sb->kqs', update_left, row_basis, precision=highest)
        orig_basis = jnp.einsum('qb,sb->qs', orig_float, row_basis, precision=highest)
        own_core = jnp.einsum('qb,qs->sb', right_orig.astype(jnp.float32), orig_basis, precision=highest)
        return own_core - jnp.einsum('kqb,kqs->sb', pivot_float, projected, precision=highest)
    cores = lax.map(one_tile, (tile_left, tile_right, tile_mask, orig_left, orig_right))
    tile_count, rank_rows, cell_count = cores.shape
    right_sides = cores.reshape(tile_count * rank_rows, cell_count).T
    solution = jax.scipy.linalg.solve_triangular(pivot_factor, right_sides, lower=True)
    return solution.T.reshape(tile_count, rank_rows, cell_count)
```

```python
from functools import partial

import jax
import jax.numpy as jnp
from jax import lax
from jax.experimental import pallas as pl
from jax.experimental.pallas import tpu as pltpu
from jax.sharding import PartitionSpec as P

HIGHEST = lax.Precision.HIGHEST
F32 = jnp.float32
BF16 = jnp.bfloat16
NN = (((1,), (0,)), ((), ()))
NT = (((1,), (1,)), ((), ()))
TN = (((0,), (0,)), ((), ()))


def dot(a, b, dims, precision=None):
    return lax.dot_general(a, b, dims, precision=precision, preferred_element_type=F32)


def split(x):
    high = x.astype(BF16)
    return high, (x - high.astype(F32)).astype(BF16)


def dot3(a, b, dims):
    (ah, al), (bh, bl) = a, b
    return dot(ah, bh, dims) + (dot(ah, bl, dims) + dot(al, bh, dims))


def owners(tiles, layers):
    base, extra = divmod(tiles, layers)
    order = sorted(range(layers), key=lambda i: abs(2 * i - layers + 1))
    count = [base + (order.index(i) < extra) for i in range(layers)]
    first = [sum(count[:i]) for i in range(layers)]
    return count, first


def pick(table, index):
    value = jnp.int32(table[0])
    for i in range(1, len(table)):
        value = jnp.where(index == i, jnp.int32(table[i]), value)
    return value


def invert_lower(block, size, stop):
    rows = lax.broadcasted_iota(jnp.int32, (size, size), 0)
    cols = lax.broadcasted_iota(jnp.int32, (size, size), 1)
    eye = rows == cols
    inverse = jnp.where(eye, 1.0 / jnp.where(eye, block, 1.0), 0.0)
    step = 1
    while step < stop:
        pair = (rows // (2 * step) == cols // (2 * step)) & (rows // step > cols // step)
        below = jnp.where(pair, block, 0.0)
        inverse = inverse - dot(inverse, dot(below, inverse, NN, HIGHEST), NN, HIGHEST)
        step *= 2
    return inverse


def eliminate(augmented, rank):
    done = []
    left = augmented
    for block in range(rank // 8):
        index = lax.broadcasted_iota(jnp.int32, (left.shape[0], left.shape[1], 1), 1)
        for at in range(8):
            column = block * 8 + at
            pivot = left[:, at : at + 1, :]
            scale = 1.0 / pivot[:, :, column : column + 1]
            weight = jnp.where(index > at, left[:, :, column : column + 1] * scale, 0.0)
            left = left - weight * pivot
        done.append(left[:, :8, :])
        left = left[:, 8:, :]
    whole = jnp.concatenate(done, axis=1)
    lanes = lax.broadcasted_iota(jnp.int32, whole.shape, 2)
    index = lax.broadcasted_iota(jnp.int32, whole.shape, 1)
    diagonal = jnp.sum(jnp.where(lanes == index, whole, 0.0), axis=2, keepdims=True)
    return whole * lax.rsqrt(diagonal)


def kernel(
    layers, rows, mask_ref, tl_ref, tr_ref, ol_ref, or_ref, pl_ref, pr_ref, sk_ref, pf_ref,
    out_ref,
    prw, plw, pw, zbuf, ce, cebuf, fbuf, mall, diag, core,
    pr_send, pr_recv, pl_send, pl_recv, pz_send, pf_send, p3_send, p_recv,
    plz_send, plf_send, tl_send, tl_recv, ce_send, ce_recv, m_send, m_recv,
):
    layer, row = lax.axis_index("layer"), lax.axis_index("row")
    tiles, rank, width = tl_ref.shape
    piece = pl_ref.shape[1]
    strip = pf_ref.shape[0]
    count, first = owners(tiles, layers)
    slots = max(count)
    chips = rows // 2
    sibling = row + 1 - 2 * lax.rem(row, 2)

    def other_layer(d):
        return lax.rem(layer + d, layers)

    def other_row(d):
        return lax.rem(row + d, rows)

    def to(l, r):
        return {"layer": l, "row": r}

    def send(src, dst, send_sem, recv_sem, device):
        return pltpu.make_async_remote_copy(
            src_ref=src, dst_ref=dst, send_sem=send_sem, recv_sem=recv_sem,
            device_id=device, device_id_type=pl.DeviceIdType.MESH,
        )

    def here(dst, sem):
        send(dst, dst, sem, sem, to(layer, sibling)).wait_recv()

    def sent(src, sem):
        send(src, src, sem, sem, to(layer, sibling)).wait_send()

    def pl_piece(l, r):
        return plw.at[l, :, pl.ds(pl.multiple_of(r * piece, piece), piece)]

    def pr_piece(r):
        return prw.at[:, pl.ds(pl.multiple_of(r * piece, piece), piece)]

    def p_strip(l, r):
        used = (l + 1) * rows * strip
        used = min(width, -(-used // 128) * 128)
        start = pl.multiple_of((l * rows + r) * strip, strip)
        return pw.at[pl.ds(start, strip), pl.ds(0, used)]

    barrier = pltpu.get_barrier_semaphore()
    for d in range(1, layers):
        pl.semaphore_signal(
            barrier, inc=1, device_id=to(other_layer(d), row), device_id_type=pl.DeviceIdType.MESH
        )
    for d in range(1, rows):
        pl.semaphore_signal(
            barrier, inc=1, device_id=to(layer, other_row(d)), device_id_type=pl.DeviceIdType.MESH
        )
    mine = pl.ds(pl.multiple_of(row * piece, piece), piece)
    prw[:, mine] = pr_ref[...]
    plw[layer, :, mine] = pl_ref[...]
    own_rows = pl.ds(pl.multiple_of((layer * rows + row) * strip, strip), strip)
    pw[own_rows, :] = pf_ref[...]
    pl.semaphore_wait(barrier, layers + rows - 2)

    for d in range(1, rows):
        send(pr_piece(row), pr_piece(row), pr_send.at[d], pr_recv.at[row], to(layer, other_row(d))).start()
        send(
            pl_piece(layer, row), pl_piece(layer, row), pl_send.at[d], pl_recv.at[layer, row],
            to(layer, other_row(d)),
        ).start()
    for d in range(1, layers):
        send(
            pl_piece(layer, row), pl_piece(layer, row), plz_send.at[d], pl_recv.at[layer, row],
            to(other_layer(d), row),
        ).start()
    for l in range(layers):

        @pl.when(layer == l)
        def _():
            for d in range(1, layers):
                send(
                    p_strip(l, row), p_strip(l, row), pz_send.at[d], p_recv.at[l, row],
                    to(other_layer(d), row),
                ).start()
            for d in range(1, chips):
                send(
                    p_strip(l, row), p_strip(l, row), pf_send.at[l, d], p_recv.at[l, row],
                    to(layer, other_row(2 * d)),
                ).start()

    for l in range(layers):
        for s in range(count[l]):
            t = first[l] + s

            @pl.when(layer != l)
            def _():
                send(
                    tl_ref.at[t], zbuf.at[s, layer + 1], tl_send.at[t], tl_recv.at[s, layer], to(l, row)
                ).start()

            @pl.when(layer == l)
            def _():
                zbuf[s, layer + 1] = tl_ref[t]

    fbuf[...] = jnp.zeros_like(fbuf)
    own_count, own_first = pick(count, layer), pick(first, layer)
    eye = (
        lax.broadcasted_iota(jnp.int32, (rank, rank), 0) == lax.broadcasted_iota(jnp.int32, (rank, rank), 1)
    ).astype(F32)
    for s in range(slots):
        t = own_first + jnp.minimum(s, own_count - 1)
        zbuf[s, 0] = ol_ref[t]
        fbuf[s, 0:rank, 0:rank] = dot(or_ref[t], sk_ref[...], NT)
        fbuf[s, 0:rank, rank : 2 * rank] = eye

    for d in range(1, rows):
        here(pr_piece(other_row(d)), pr_recv.at[other_row(d)])
        here(pl_piece(layer, other_row(d)), pl_recv.at[layer, other_row(d)])
    coupling = dot(tr_ref[...].reshape(tiles * rank, width), prw[...], NT)
    sketched = dot(plw[layer], sk_ref[...], NT)
    chained = dot(coupling, sketched, NN, HIGHEST)
    for t in range(tiles):
        weight = -(mask_ref[t, 0].astype(F32))
        block = slice(t * rank, (t + 1) * rank)
        ce[t, :, 0:rank] = chained[block] * weight
        ce[t, :, rank : 2 * rank] = coupling[block] * weight
    for l in range(layers):
        for s in range(count[l]):
            t = first[l] + s

            @pl.when(layer != l)
            def _():
                send(
                    ce.at[t], cebuf.at[s, layer], ce_send.at[t], ce_recv.at[s, layer], to(l, row)
                ).start()

            @pl.when(layer == l)
            def _():
                cebuf[s, layer] = ce[t]

    for l in range(layers):

        @pl.when(layer != l)
        def _():
            here(pl_piece(l, row), pl_recv.at[l, row])
            for d in range(1, rows):
                send(
                    pl_piece(l, row), pl_piece(l, row), plf_send.at[l, d], pl_recv.at[l, row],
                    to(layer, other_row(d)),
                ).start()
            here(p_strip(l, row), p_recv.at[l, row])
            for d in range(1, chips):
                send(
                    p_strip(l, row), p_strip(l, row), pf_send.at[l, d], p_recv.at[l, row],
                    to(layer, other_row(2 * d)),
                ).start()

    for d in range(chips):
        for l in range(layers):
            r = other_row(2 * d)
            if d:
                here(p_strip(l, r), p_recv.at[l, r])
            send(
                p_strip(l, r), p_strip(l, r), p3_send.at[l, d], p_recv.at[l, r], to(layer, sibling)
            ).start()

    for l in range(layers):

        @pl.when(layer == l)
        def _():
            for s in range(count[l]):
                for k in range(layers):
                    if k != l:
                        here(zbuf.at[s, k + 1], tl_recv.at[s, k])
                        here(cebuf.at[s, k], ce_recv.at[s, k])

    parts = []
    for s in range(slots):
        at = jnp.minimum(s, own_count - 1)
        z = zbuf[at].reshape((layers + 1) * rank, width)
        gram = dot(z, z, NT)
        for k in range(layers):
            block = slice((k + 1) * rank, (k + 2) * rank)
            fbuf[s, block, 0:rank] = cebuf[at, k, :, 0:rank]
            fbuf[s, block, (k + 2) * rank : (k + 3) * rank] = cebuf[at, k, :, rank : 2 * rank]
        joined = dot(fbuf[s, :, 0:rank], gram, TN, HIGHEST)
        parts.append(dot(joined, fbuf[s], NN, HIGHEST)[None])
    found = eliminate(jnp.concatenate(parts, axis=0), rank)
    for l in range(layers):

        @pl.when(layer == l)
        def _():
            for s in range(count[l]):
                t = first[l] + s
                mall[t] = found[s]
                for d in range(1, layers):
                    send(
                        mall.at[t], mall.at[t], m_send.at[t, d], m_recv.at[t], to(other_layer(d), row)
                    ).start()

    for l in range(layers):
        for d in range(chips):
            r = lax.rem(sibling + 2 * d, rows)
            here(p_strip(l, r), p_recv.at[l, r])
    chunk = 256
    half = chunk // 2
    for c in range(width // chunk):
        lo, mid, hi = c * chunk, c * chunk + half, (c + 1) * chunk
        top = invert_lower(pw[lo:mid, lo:mid], half, half)
        bottom = invert_lower(pw[mid:hi, mid:hi], half, half)
        cross = dot(bottom, dot(pw[mid:hi, lo:mid], top, NN, HIGHEST), NN, HIGHEST)
        diag[c, 0:half, 0:half] = top
        diag[c, 0:half, half:chunk] = jnp.zeros_like(top)
        diag[c, half:chunk, 0:half] = -cross
        diag[c, half:chunk, half:chunk] = bottom

    for l in range(layers):

        @pl.when(layer != l)
        def _():
            for d in range(1, rows):
                here(pl_piece(l, other_row(d)), pl_recv.at[l, other_row(d)])
            for s in range(count[l]):
                here(mall.at[first[l] + s], m_recv.at[first[l] + s])

    panels = plw[...].reshape(layers * rank, width)
    for t in range(tiles):
        high, low = split(mall[t, :, rank : 2 * rank])
        core[t * rank : (t + 1) * rank, :] = dot(high, or_ref[t], NN) + dot(low, or_ref[t], NN)
    high, low = split(mall[:, :, 2 * rank :].reshape(tiles * rank, layers * rank))
    solved = []
    for c in range(width // chunk):
        cols = slice(c * chunk, (c + 1) * chunk)
        rest = core[:, cols] + (dot(high, panels[:, cols], NN) + dot(low, panels[:, cols], NN))
        for i in range(c):
            rest = rest - dot3(solved[i], split(pw[cols, i * chunk : (i + 1) * chunk]), NT)
        x = dot3(split(rest), split(diag[c]), NT)
        out_ref[:, :, cols] = x.reshape(tiles, rank, chunk)
        solved.append(split(x))

    for d in range(1, rows):
        sent(pr_piece(row), pr_send.at[d])
        sent(pl_piece(layer, row), pl_send.at[d])
    for d in range(1, layers):
        sent(pl_piece(layer, row), plz_send.at[d])
    for l in range(layers):
        for d in range(1, chips):
            sent(p_strip(l, row), pf_send.at[l, d])
        for d in range(chips):
            sent(p_strip(l, other_row(2 * d)), p3_send.at[l, d])

        @pl.when(layer == l)
        def _():
            for d in range(1, layers):
                sent(p_strip(l, row), pz_send.at[d])
                for s in range(count[l]):
                    sent(mall.at[first[l] + s], m_send.at[first[l] + s, d])

        @pl.when(layer != l)
        def _():
            for d in range(1, rows):
                sent(pl_piece(l, row), plf_send.at[l, d])
            for s in range(count[l]):
                sent(tl_ref.at[first[l] + s], tl_send.at[first[l] + s])
                sent(ce.at[first[l] + s], ce_send.at[first[l] + s])


def shards_kernel(layers, rows, tile_left, tile_right, tile_mask, orig_left, orig_right, pivot_left, pivot_right, sketch, pivot_factor):
    tiles, _, rank, width = tile_left.shape
    slots = max(owners(tiles, layers)[0])
    dma = pltpu.SemaphoreType.DMA
    vmem = pl.BlockSpec(memory_space=pltpu.VMEM)
    lanes = (layers + 2) * rank
    return pl.pallas_call(
        partial(kernel, layers, rows),
        out_shape=jax.ShapeDtypeStruct((tiles, rank, width), F32),
        in_specs=[pl.BlockSpec(memory_space=pltpu.SMEM)] + [vmem] * 8,
        out_specs=vmem,
        scratch_shapes=[
            pltpu.VMEM((rank, width), BF16),
            pltpu.VMEM((layers, rank, width), BF16),
            pltpu.VMEM((width, width), F32),
            pltpu.VMEM((slots, layers + 1, rank, width), BF16),
            pltpu.VMEM((tiles, rank, 2 * rank), F32),
            pltpu.VMEM((slots, layers, rank, 2 * rank), F32),
            pltpu.VMEM((slots, (layers + 1) * rank, lanes), F32),
            pltpu.VMEM((tiles, rank, lanes), F32),
            pltpu.VMEM((width // 256, 256, 256), F32),
            pltpu.VMEM((tiles * rank, width), F32),
            dma((rows,)), dma((rows,)), dma((rows,)), dma((layers, rows)),
            dma((layers,)), dma((layers, rows)), dma((layers, rows)), dma((layers, rows)),
            dma((layers,)), dma((layers, rows)),
            dma((tiles,)), dma((slots, layers)), dma((tiles,)), dma((slots, layers)),
            dma((tiles, layers)), dma((tiles,)),
        ],
        compiler_params=pltpu.CompilerParams(
            collective_id=0, has_side_effects=True, vmem_limit_bytes=50 * 1024 * 1024
        ),
    )(
        tile_mask, tile_left.reshape(tiles, rank, width), tile_right.reshape(tiles, rank, width),
        orig_left, orig_right, pivot_left.reshape(rank, -1), pivot_right.reshape(rank, -1),
        sketch, pivot_factor,
    )


def shards_general(
    tile_left,
    tile_right,
    tile_mask,
    orig_left,
    orig_right,
    pivot_left,
    pivot_right,
    sketch,
    pivot_factor,
):
    highest = HIGHEST
    pivot_whole = lax.all_gather(pivot_factor, ("layer", "row"), axis=0, tiled=True)
    left_whole, right_whole = (
        lax.all_gather(pivot_left, "row", axis=2, tiled=True),
        lax.all_gather(pivot_right, "row", axis=2, tiled=True),
    )
    coupling = jnp.einsum("tpqb,psb->tpqs", tile_right, right_whole, preferred_element_type=F32)
    weights = tile_mask.astype(F32)[:, :, None, None]
    update_left = jnp.einsum("tpqs,tpqb->tpsb", coupling, tile_left.astype(F32), precision=highest) * weights
    sketched = jnp.einsum("pqb,sb->pqs", left_whole, sketch, preferred_element_type=F32)
    partial_sample = jnp.einsum("tpqb,pqs->tsb", update_left, sketched, precision=highest)
    orig_float = orig_left.astype(F32)
    orig_sketch = jnp.einsum("tqb,sb->tqs", orig_right, sketch, preferred_element_type=F32)
    own_sample = jnp.einsum("tqb,tqs->tsb", orig_float, orig_sketch, precision=highest)
    sample = own_sample - lax.psum(partial_sample, "layer")
    gram_matrix = jnp.einsum("tqb,tsb->tqs", sample, sample, precision=highest)
    factor = jnp.linalg.cholesky(gram_matrix)
    row_basis = jax.vmap(partial(jax.scipy.linalg.solve_triangular, lower=True))(factor, sample)
    projected = jnp.einsum("tpqb,tsb->tpqs", update_left, row_basis, precision=highest)
    partial_core = jnp.einsum("pqb,tpqs->tsb", left_whole.astype(F32), projected, precision=highest)
    orig_basis = jnp.einsum("tqb,tsb->tqs", orig_float, row_basis, precision=highest)
    own_core = jnp.einsum("tqb,tqs->tsb", orig_right.astype(F32), orig_basis, precision=highest)
    core = own_core - lax.psum(partial_core, "layer")
    tile_count, rank_rows, cell_count = core.shape
    right_sides = core.reshape(tile_count * rank_rows, cell_count).T
    solution = jax.scipy.linalg.solve_triangular(pivot_whole, right_sides, lower=True)
    return solution.T.reshape(tile_count, rank_rows, cell_count)


def solution(mesh):
    in_specs = (
        P("row", "layer", None, None),
        P("row", "layer", None, None),
        P("row", "layer"),
        P("row", None, None),
        P("row", None, None),
        P("layer", None, "row"),
        P("layer", None, "row"),
        P(),
        P(("layer", "row"), None),
    )
    out_specs = P("row", None, None)
    layers, rows = mesh.shape["layer"], mesh.shape["row"]

    def shards(*blocks):
        tiles, panels, rank, width = blocks[0].shape
        fits = (
            panels == 1 and tiles >= layers and rank == 64 and width % 256 == 0 and rows % 2 == 0
            and width % (128 * rows) == 0 and width % (8 * layers * rows) == 0
        )
        if fits:
            return shards_kernel(layers, rows, *blocks)
        return shards_general(*blocks)

    return jax.shard_map(shards, mesh=mesh, in_specs=in_specs, out_specs=out_specs, check_vma=False)
```

```python
from functools import partial

import jax
import jax.numpy as jnp
from jax import lax
from jax.experimental import pallas as pl
from jax.experimental.pallas import tpu as pltpu
from jax.sharding import PartitionSpec as P

HIGHEST = lax.Precision.HIGHEST
F32 = jnp.float32
BF16 = jnp.bfloat16
NN = (((1,), (0,)), ((), ()))
NT = (((1,), (1,)), ((), ()))
TN = (((0,), (0,)), ((), ()))


def dot(a, b, dims, precision=None):
    return lax.dot_general(a, b, dims, precision=precision, preferred_element_type=F32)


def split(x):
    high = x.astype(BF16)
    return high, (x - high.astype(F32)).astype(BF16)


def dot3(a, b, dims):
    (ah, al), (bh, bl) = a, b
    return dot(ah, bh, dims) + (dot(ah, bl, dims) + dot(al, bh, dims))


def owners(tiles, layers):
    base, extra = divmod(tiles, layers)
    order = sorted(range(layers), key=lambda i: abs(2 * i - layers + 1))
    count = [base + (order.index(i) < extra) for i in range(layers)]
    first = [sum(count[:i]) for i in range(layers)]
    return count, first


def pick(table, index):
    value = jnp.int32(table[0])
    for i in range(1, len(table)):
        value = jnp.where(index == i, jnp.int32(table[i]), value)
    return value


def invert_lower(blocks, size):
    rows = lax.broadcasted_iota(jnp.int32, (size, size), 0)
    cols = lax.broadcasted_iota(jnp.int32, (size, size), 1)
    eye = rows == cols
    inverses = [jnp.where(eye, 1.0 / jnp.where(eye, block, 1.0), 0.0) for block in blocks]
    step = 1
    while step < size:
        pair = (rows // (2 * step) == cols // (2 * step)) & (rows // step > cols // step)
        inner = [
            dot(jnp.where(pair, block, 0.0), inverse, NN, HIGHEST) for block, inverse in zip(blocks, inverses)
        ]
        outer = [dot(inverse, right, NN, HIGHEST) for inverse, right in zip(inverses, inner)]
        inverses = [inverse - change for inverse, change in zip(inverses, outer)]
        step *= 2
    return inverses


def eliminate(augmented, rank):
    lanes = 128
    tiles = [augmented[:, :, i : i + lanes] for i in range(0, augmented.shape[2], lanes)]
    done = [[] for _ in tiles]
    roots = []
    for block in range(rank // 8):
        shape = tiles[0].shape
        index = lax.broadcasted_iota(jnp.int32, shape, 1)
        columns = [
            jnp.broadcast_to(tiles[0][:, :, block * 8 + at : block * 8 + at + 1], shape) for at in range(8)
        ]
        for at in range(8):
            pivot = columns[at][:, at : at + 1, :]
            weight = jnp.where(index > at, columns[at] * (1.0 / pivot), 0.0)
            for later in range(at + 1, 8):
                columns[later] = columns[later] - weight * columns[later][:, at : at + 1, :]
            tiles = [tile - weight * tile[:, at : at + 1, :] for tile in tiles]
            roots.append(lax.rsqrt(pivot))
        for i, tile in enumerate(tiles):
            done[i].append(tile[:, :8, :])
        tiles = [tile[:, 8:, :] for tile in tiles]
    scale = jnp.concatenate(roots, axis=1)
    return jnp.concatenate([jnp.concatenate(part, axis=1) * scale for part in done], axis=2)


def kernel(
    layers, rows, mask_ref, tl_ref, tr_ref, ol_ref, or_ref, pl_ref, pr_ref, sk_ref, pf_ref,
    out_ref,
    prw, plw, pw, zbuf, ce, cebuf, fbuf, mall, diag, below, core, trv, orv, skv, xv,
    pr_send, pr_recv, pl_send, pl_recv, pz_send, pf_send, p3_send, p_recv,
    plz_send, plf_send, tl_send, tl_recv, ce_send, ce_recv, m_send, m_recv, load, local, leave,
):
    layer, row = lax.axis_index("layer"), lax.axis_index("row")
    tiles, rank, width = tl_ref.shape
    piece = pl_ref.shape[1]
    strip = pf_ref.shape[0]
    count, first = owners(tiles, layers)
    slots = max(count)
    chips = rows // 2
    sibling = row + 1 - 2 * lax.rem(row, 2)

    def other_layer(d):
        return lax.rem(layer + d, layers)

    def other_row(d):
        return lax.rem(row + d, rows)

    def to(l, r):
        return {"layer": l, "row": r}

    def send(src, dst, send_sem, recv_sem, device):
        return pltpu.make_async_remote_copy(
            src_ref=src, dst_ref=dst, send_sem=send_sem, recv_sem=recv_sem,
            device_id=device, device_id_type=pl.DeviceIdType.MESH,
        )

    def here(dst, sem):
        send(dst, dst, sem, sem, to(layer, sibling)).wait_recv()

    def sent(src, sem):
        send(src, src, sem, sem, to(layer, sibling)).wait_send()

    def pl_piece(l, r):
        return plw.at[l, :, pl.ds(pl.multiple_of(r * piece, piece), piece)]

    def pr_piece(r):
        return prw.at[:, pl.ds(pl.multiple_of(r * piece, piece), piece)]

    def used(l):
        return min(width, -(-((l + 1) * rows * strip) // 128) * 128)

    def p_strip(l, r):
        start = pl.multiple_of((l * rows + r) * strip, strip)
        return pw.at[pl.ds(start, strip), pl.ds(0, used(l))]

    def own_strip(l):
        return pf_ref.at[:, pl.ds(0, used(l))]

    barrier = pltpu.get_barrier_semaphore()
    for d in range(1, layers):
        pl.semaphore_signal(
            barrier, inc=1, device_id=to(other_layer(d), row), device_id_type=pl.DeviceIdType.MESH
        )
    for d in range(1, rows):
        pl.semaphore_signal(
            barrier, inc=1, device_id=to(layer, other_row(d)), device_id_type=pl.DeviceIdType.MESH
        )
    own_count, own_first = pick(count, layer), pick(first, layer)
    own_rows = pl.ds(pl.multiple_of((layer * rows + row) * strip, strip), strip)
    loads = [
        pltpu.make_async_copy(src, dst, load.at[i])
        for i, (src, dst) in enumerate([
            (pr_ref, pr_piece(row)), (pl_ref, pl_piece(layer, row)), (sk_ref, skv), (tr_ref, trv),
            (or_ref, orv), (pf_ref, pw.at[own_rows, :]),
        ])
    ]
    for s in range(slots):
        t = own_first + jnp.minimum(s, own_count - 1)
        loads.append(pltpu.make_async_copy(ol_ref.at[t], zbuf.at[s, 0], local.at[0, s]))
        loads.append(pltpu.make_async_copy(tl_ref.at[t], zbuf.at[s, layer + 1], local.at[1, s]))
    for copy in loads:
        copy.start()
    pl.semaphore_wait(barrier, layers + rows - 2)

    for d in range(1, rows):
        send(pr_ref, pr_piece(row), pr_send.at[d], pr_recv.at[row], to(layer, other_row(d))).start()
        send(
            pl_ref, pl_piece(layer, row), pl_send.at[d], pl_recv.at[layer, row],
            to(layer, other_row(d)),
        ).start()
    for d in range(1, layers):
        send(
            pl_ref, pl_piece(layer, row), plz_send.at[d], pl_recv.at[layer, row],
            to(other_layer(d), row),
        ).start()
    for l in range(layers):

        @pl.when(layer == l)
        def _():
            for d in range(1, layers):
                send(
                    own_strip(l), p_strip(l, row), pz_send.at[d], p_recv.at[l, row],
                    to(other_layer(d), row),
                ).start()
            for d in range(1, chips):
                send(
                    own_strip(l), p_strip(l, row), pf_send.at[l, d], p_recv.at[l, row],
                    to(layer, other_row(2 * d)),
                ).start()

    for l in range(layers):
        for s in range(count[l]):
            t = first[l] + s

            @pl.when(layer != l)
            def _():
                send(
                    tl_ref.at[t], zbuf.at[s, layer + 1], tl_send.at[t], tl_recv.at[s, layer], to(l, row)
                ).start()

    fbuf[...] = jnp.zeros_like(fbuf)
    eye = (
        lax.broadcasted_iota(jnp.int32, (rank, rank), 0) == lax.broadcasted_iota(jnp.int32, (rank, rank), 1)
    ).astype(F32)
    for copy in loads:
        copy.wait()
    for s in range(slots):
        t = own_first + jnp.minimum(s, own_count - 1)
        fbuf[s, 0:rank, 0:rank] = dot(orv[t], skv[...], NT)
        fbuf[s, 0:rank, rank : 2 * rank] = eye

    for d in range(1, rows):
        here(pr_piece(other_row(d)), pr_recv.at[other_row(d)])
        here(pl_piece(layer, other_row(d)), pl_recv.at[layer, other_row(d)])
    coupling = dot(trv[...].reshape(tiles * rank, width), prw[...], NT)
    sketched = dot(plw[layer], skv[...], NT)
    chained = dot(coupling, sketched, NN, HIGHEST)
    for t in range(tiles):
        weight = -(mask_ref[t, 0].astype(F32))
        block = slice(t * rank, (t + 1) * rank)
        ce[t, :, 0:rank] = chained[block] * weight
        ce[t, :, rank : 2 * rank] = coupling[block] * weight
    for l in range(layers):
        for s in range(count[l]):
            t = first[l] + s

            @pl.when(layer != l)
            def _():
                send(
                    ce.at[t], cebuf.at[s, layer], ce_send.at[t], ce_recv.at[s, layer], to(l, row)
                ).start()

            @pl.when(layer == l)
            def _():
                cebuf[s, layer] = ce[t]

    for l in range(layers):

        @pl.when(layer != l)
        def _():
            here(pl_piece(l, row), pl_recv.at[l, row])
            for d in range(1, rows):
                send(
                    pl_piece(l, row), pl_piece(l, row), plf_send.at[l, d], pl_recv.at[l, row],
                    to(layer, other_row(d)),
                ).start()
            here(p_strip(l, row), p_recv.at[l, row])
            for d in range(1, chips):
                send(
                    p_strip(l, row), p_strip(l, row), pf_send.at[l, d], p_recv.at[l, row],
                    to(layer, other_row(2 * d)),
                ).start()

    for d in range(chips):
        for l in range(layers):
            r = other_row(2 * d)
            if d:
                here(p_strip(l, r), p_recv.at[l, r])
            send(
                p_strip(l, r), p_strip(l, r), p3_send.at[l, d], p_recv.at[l, r], to(layer, sibling)
            ).start()

    for l in range(layers):

        @pl.when(layer == l)
        def _():
            for s in range(count[l]):
                for k in range(layers):
                    if k != l:
                        here(zbuf.at[s, k + 1], tl_recv.at[s, k])
                        here(cebuf.at[s, k], ce_recv.at[s, k])

    parts = []
    for s in range(slots):
        at = jnp.minimum(s, own_count - 1)
        z = zbuf[at].reshape((layers + 1) * rank, width)
        gram = dot(z, z, NT)
        for k in range(layers):
            block = slice((k + 1) * rank, (k + 2) * rank)
            fbuf[s, block, 0:rank] = cebuf[at, k, :, 0:rank]
            fbuf[s, block, (k + 2) * rank : (k + 3) * rank] = cebuf[at, k, :, rank : 2 * rank]
        joined = dot(fbuf[s, :, 0:rank], gram, TN, HIGHEST)
        parts.append(dot(joined, fbuf[s], NN, HIGHEST)[None])
    found = eliminate(jnp.concatenate(parts, axis=0), rank)
    for l in range(layers):

        @pl.when(layer == l)
        def _():
            for s in range(count[l]):
                t = first[l] + s
                high, low = split(found[s][:, rank:])
                mall[t, :, 0:rank] = high[:, 0:rank]
                mall[t, :, rank : 2 * rank] = low[:, 0:rank]
                mall[t, :, 2 * rank : (layers + 2) * rank] = high[:, rank:]
                mall[t, :, (layers + 2) * rank :] = low[:, rank:]
                for d in range(1, layers):
                    send(
                        mall.at[t], mall.at[t], m_send.at[t, d], m_recv.at[t], to(other_layer(d), row)
                    ).start()

    for l in range(layers):
        for d in range(chips):
            r = lax.rem(sibling + 2 * d, rows)
            here(p_strip(l, r), p_recv.at[l, r])
    chunk = 256
    half = chunk // 2
    chunks = width // chunk
    inverses = invert_lower(
        [pw[i * half : (i + 1) * half, i * half : (i + 1) * half] for i in range(2 * chunks)], half
    )
    inner = [
        dot(pw[c * chunk + half : (c + 1) * chunk, c * chunk : c * chunk + half], inverses[2 * c], NN, HIGHEST)
        for c in range(chunks)
    ]
    for c in range(chunks):
        cross = dot(inverses[2 * c + 1], inner[c], NN, HIGHEST)
        for part, value in enumerate(split(inverses[2 * c])):
            diag[part, c, 0:half, 0:half] = value
        for part, value in enumerate(split(inverses[2 * c + 1])):
            diag[part, c, half:chunk, half:chunk] = value
        for part, value in enumerate(split(-cross)):
            diag[part, c, half:chunk, 0:half] = value
            diag[part, c, 0:half, half:chunk] = jnp.zeros_like(value)
        if c:
            rows_at = slice(c * chunk, (c + 1) * chunk)
            for part, value in enumerate(split(pw[rows_at, 0 : c * chunk])):
                below[part, rows_at, 0 : c * chunk] = value

    for l in range(layers):

        @pl.when(layer != l)
        def _():
            for d in range(1, rows):
                here(pl_piece(l, other_row(d)), pl_recv.at[l, other_row(d)])
            for s in range(count[l]):
                here(mall.at[first[l] + s], m_recv.at[first[l] + s])

    panels = plw[...].reshape(layers * rank, width)
    for t in range(tiles):
        core[t * rank : (t + 1) * rank, :] = dot(mall[t, :, 0:rank], orv[t], NN) + dot(
            mall[t, :, rank : 2 * rank], orv[t], NN
        )
    high = mall[:, :, 2 * rank : (layers + 2) * rank].reshape(tiles * rank, layers * rank)
    low = mall[:, :, (layers + 2) * rank :].reshape(tiles * rank, layers * rank)
    solved = []
    outs = []
    for c in range(chunks):
        cols = slice(c * chunk, (c + 1) * chunk)
        rest = core[:, cols] + (dot(high, panels[:, cols], NN) + dot(low, panels[:, cols], NN))
        for i in range(c):
            at = slice(i * chunk, (i + 1) * chunk)
            rest = rest - dot3(solved[i], (below[0, cols, at], below[1, cols, at]), NT)
        x = dot3(split(rest), (diag[0, c], diag[1, c]), NT)
        xv[:, :, cols] = x.reshape(tiles, rank, chunk)
        outs.append(
            pltpu.make_async_copy(
                xv.at[:, :, pl.ds(c * chunk, chunk)], out_ref.at[:, :, pl.ds(c * chunk, chunk)], leave.at[c]
            )
        )
        outs[-1].start()
        if c + 1 < chunks:
            solved.append(split(x))

    for copy in outs:
        copy.wait()
    for d in range(1, rows):
        sent(pr_piece(row), pr_send.at[d])
        sent(pl_piece(layer, row), pl_send.at[d])
    for d in range(1, layers):
        sent(pl_piece(layer, row), plz_send.at[d])
    for l in range(layers):
        for d in range(1, chips):
            sent(p_strip(l, row), pf_send.at[l, d])
        for d in range(chips):
            sent(p_strip(l, other_row(2 * d)), p3_send.at[l, d])

        @pl.when(layer == l)
        def _():
            for d in range(1, layers):
                sent(p_strip(l, row), pz_send.at[d])
                for s in range(count[l]):
                    sent(mall.at[first[l] + s], m_send.at[first[l] + s, d])

        @pl.when(layer != l)
        def _():
            for d in range(1, rows):
                sent(pl_piece(l, row), plf_send.at[l, d])
            for s in range(count[l]):
                sent(tl_ref.at[first[l] + s], tl_send.at[first[l] + s])
                sent(ce.at[first[l] + s], ce_send.at[first[l] + s])


def shards_kernel(layers, rows, tile_left, tile_right, tile_mask, orig_left, orig_right, pivot_left, pivot_right, sketch, pivot_factor):
    tiles, _, rank, width = tile_left.shape
    slots = max(owners(tiles, layers)[0])
    dma = pltpu.SemaphoreType.DMA
    hbm = pl.BlockSpec(memory_space=pl.ANY)
    lanes = (layers + 2) * rank
    return pl.pallas_call(
        partial(kernel, layers, rows),
        out_shape=jax.ShapeDtypeStruct((tiles, rank, width), F32),
        in_specs=[pl.BlockSpec(memory_space=pltpu.SMEM)] + [hbm] * 8,
        out_specs=hbm,
        scratch_shapes=[
            pltpu.VMEM((rank, width), BF16),
            pltpu.VMEM((layers, rank, width), BF16),
            pltpu.VMEM((width, width), F32),
            pltpu.VMEM((slots, layers + 1, rank, width), BF16),
            pltpu.VMEM((tiles, rank, 2 * rank), F32),
            pltpu.VMEM((slots, layers, rank, 2 * rank), F32),
            pltpu.VMEM((slots, (layers + 1) * rank, lanes), F32),
            pltpu.VMEM((tiles, rank, 2 * (layers + 1) * rank), BF16),
            pltpu.VMEM((2, width // 256, 256, 256), BF16),
            pltpu.VMEM((2, width, width), BF16),
            pltpu.VMEM((tiles * rank, width), F32),
            pltpu.VMEM((tiles, rank, width), BF16),
            pltpu.VMEM((tiles, rank, width), BF16),
            pltpu.VMEM((rank, width), BF16),
            pltpu.VMEM((tiles, rank, width), F32),
            dma((rows,)), dma((rows,)), dma((rows,)), dma((layers, rows)),
            dma((layers,)), dma((layers, rows)), dma((layers, rows)), dma((layers, rows)),
            dma((layers,)), dma((layers, rows)),
            dma((tiles,)), dma((slots, layers)), dma((tiles,)), dma((slots, layers)),
            dma((tiles, layers)), dma((tiles,)), dma((6,)), dma((2, slots)), dma((width // 256,)),
        ],
        compiler_params=pltpu.CompilerParams(
            collective_id=0, has_side_effects=True, vmem_limit_bytes=50 * 1024 * 1024
        ),
    )(
        tile_mask, tile_left.reshape(tiles, rank, width), tile_right.reshape(tiles, rank, width),
        orig_left, orig_right, pivot_left.reshape(rank, -1), pivot_right.reshape(rank, -1),
        sketch, pivot_factor,
    )


def shards_general(
    tile_left,
    tile_right,
    tile_mask,
    orig_left,
    orig_right,
    pivot_left,
    pivot_right,
    sketch,
    pivot_factor,
):
    highest = HIGHEST
    pivot_whole = lax.all_gather(pivot_factor, ("layer", "row"), axis=0, tiled=True)
    left_whole, right_whole = (
        lax.all_gather(pivot_left, "row", axis=2, tiled=True),
        lax.all_gather(pivot_right, "row", axis=2, tiled=True),
    )
    coupling = jnp.einsum("tpqb,psb->tpqs", tile_right, right_whole, preferred_element_type=F32)
    weights = tile_mask.astype(F32)[:, :, None, None]
    update_left = jnp.einsum("tpqs,tpqb->tpsb", coupling, tile_left.astype(F32), precision=highest) * weights
    sketched = jnp.einsum("pqb,sb->pqs", left_whole, sketch, preferred_element_type=F32)
    partial_sample = jnp.einsum("tpqb,pqs->tsb", update_left, sketched, precision=highest)
    orig_float = orig_left.astype(F32)
    orig_sketch = jnp.einsum("tqb,sb->tqs", orig_right, sketch, preferred_element_type=F32)
    own_sample = jnp.einsum("tqb,tqs->tsb", orig_float, orig_sketch, precision=highest)
    sample = own_sample - lax.psum(partial_sample, "layer")
    gram_matrix = jnp.einsum("tqb,tsb->tqs", sample, sample, precision=highest)
    factor = jnp.linalg.cholesky(gram_matrix)
    row_basis = jax.vmap(partial(jax.scipy.linalg.solve_triangular, lower=True))(factor, sample)
    projected = jnp.einsum("tpqb,tsb->tpqs", update_left, row_basis, precision=highest)
    partial_core = jnp.einsum("pqb,tpqs->tsb", left_whole.astype(F32), projected, precision=highest)
    orig_basis = jnp.einsum("tqb,tsb->tqs", orig_float, row_basis, precision=highest)
    own_core = jnp.einsum("tqb,tqs->tsb", orig_right.astype(F32), orig_basis, precision=highest)
    core = own_core - lax.psum(partial_core, "layer")
    tile_count, rank_rows, cell_count = core.shape
    right_sides = core.reshape(tile_count * rank_rows, cell_count).T
    solution = jax.scipy.linalg.solve_triangular(pivot_whole, right_sides, lower=True)
    return solution.T.reshape(tile_count, rank_rows, cell_count)


def solution(mesh):
    in_specs = (
        P("row", "layer", None, None),
        P("row", "layer", None, None),
        P("row", "layer"),
        P("row", None, None),
        P("row", None, None),
        P("layer", None, "row"),
        P("layer", None, "row"),
        P(),
        P(("layer", "row"), None),
    )
    out_specs = P("row", None, None)
    layers, rows = mesh.shape["layer"], mesh.shape["row"]

    def shards(*blocks):
        tiles, panels, rank, width = blocks[0].shape
        fits = (
            panels == 1 and tiles >= layers and rank == 64 and width % 256 == 0 and rows % 2 == 0
            and width % (128 * rows) == 0 and width % (8 * layers * rows) == 0
        )
        if fits:
            return shards_kernel(layers, rows, *blocks)
        return shards_general(*blocks)

    return jax.shard_map(shards, mesh=mesh, in_specs=in_specs, out_specs=out_specs, check_vma=False)
```

```python
from functools import partial

import jax
import jax.numpy as jnp
from jax import lax
from jax.experimental import pallas as pl
from jax.experimental.pallas import tpu as pltpu
from jax.sharding import PartitionSpec as P

HIGHEST = lax.Precision.HIGHEST
F32 = jnp.float32
BF16 = jnp.bfloat16
NN = (((1,), (0,)), ((), ()))
NT = (((1,), (1,)), ((), ()))


def dot(a, b, dims, precision=None):
    return lax.dot_general(a, b, dims, precision=precision, preferred_element_type=F32)


def split(x):
    high = x.astype(BF16)
    return high, (x - high.astype(F32)).astype(BF16)


def dot3(a, b, dims):
    (ah, al), (bh, bl) = a, b
    return dot(ah, bh, dims) + (dot(ah, bl, dims) + dot(al, bh, dims))


def split3(x):
    high = x.astype(BF16)
    rest = x - high.astype(F32)
    middle = rest.astype(BF16)
    return high, middle, (rest - middle.astype(F32)).astype(BF16)


def dot6(a, b):
    rows = a.shape[0]
    stacked = jnp.concatenate(split3(a), axis=0)
    high, middle, low = split3(b)
    by_high = dot(stacked, high, NN)
    by_middle = dot(stacked[: 2 * rows], middle, NN)
    by_low = dot(stacked[:rows], low, NN)
    small = by_high[2 * rows :] + by_middle[rows:] + by_low
    return by_high[:rows] + (by_high[rows : 2 * rows] + by_middle[:rows] + small)


def owners(tiles, layers):
    base, extra = divmod(tiles, layers)
    order = sorted(range(layers), key=lambda i: abs(2 * i - layers + 1))
    count = [base + (order.index(i) < extra) for i in range(layers)]
    first = [sum(count[:i]) for i in range(layers)]
    return count, first


def pick(table, index):
    value = jnp.int32(table[0])
    for i in range(1, len(table)):
        value = jnp.where(index == i, jnp.int32(table[i]), value)
    return value


def invert_lower(blocks, size):
    rows = lax.broadcasted_iota(jnp.int32, (size, size), 0)
    cols = lax.broadcasted_iota(jnp.int32, (size, size), 1)
    eye = rows == cols
    inverses = [jnp.where(eye, 1.0 / jnp.where(eye, block, 1.0), 0.0) for block in blocks]
    step = 1
    while step < size:
        pair = (rows // (2 * step) == cols // (2 * step)) & (rows // step > cols // step)
        inner = [
            dot(jnp.where(pair, block, 0.0), inverse, NN, HIGHEST) for block, inverse in zip(blocks, inverses)
        ]
        outer = [dot(inverse, right, NN, HIGHEST) for inverse, right in zip(inverses, inner)]
        inverses = [inverse - change for inverse, change in zip(inverses, outer)]
        step *= 2
    return inverses


def eliminate(augmented, rank):
    lanes = 128
    tiles = [augmented[:, :, i : i + lanes] for i in range(0, augmented.shape[2], lanes)]
    done = [[] for _ in tiles]
    roots = []
    for block in range(rank // 8):
        shape = tiles[0].shape
        index = lax.broadcasted_iota(jnp.int32, shape, 1)
        columns = [
            jnp.broadcast_to(tiles[0][:, :, block * 8 + at : block * 8 + at + 1], shape) for at in range(8)
        ]
        for at in range(8):
            pivot = columns[at][:, at : at + 1, :]
            weight = jnp.where(index > at, columns[at] * (1.0 / pivot), 0.0)
            for later in range(at + 1, 8):
                columns[later] = columns[later] - weight * columns[later][:, at : at + 1, :]
            tiles = [tile - weight * tile[:, at : at + 1, :] for tile in tiles]
            roots.append(lax.rsqrt(pivot))
        for i, tile in enumerate(tiles):
            done[i].append(tile[:, :8, :])
        tiles = [tile[:, 8:, :] for tile in tiles]
    scale = jnp.concatenate(roots, axis=1)
    return jnp.concatenate([jnp.concatenate(part, axis=1) * scale for part in done], axis=2)


def kernel(
    layers, rows, mask_ref, tl_ref, tr_ref, ol_ref, or_ref, pl_ref, pr_ref, sk_ref, pf_ref,
    out_ref,
    prw, plw, pw, zbuf, ce, cebuf, fbuf, mall, diag, below, core, trv, orv, skv, xv,
    pr_send, pr_recv, pl_send, pl_recv, pz_send, pf_send, p3_send, p_recv,
    plz_send, plf_send, tl_send, tl_recv, ce_send, ce_recv, m_send, m_recv, load, local, leave,
):
    layer, row = lax.axis_index("layer"), lax.axis_index("row")
    tiles, rank, width = tl_ref.shape
    piece = pl_ref.shape[1]
    strip = pf_ref.shape[0]
    count, first = owners(tiles, layers)
    slots = max(count)
    chips = rows // 2
    sibling = row + 1 - 2 * lax.rem(row, 2)

    def other_layer(d):
        return lax.rem(layer + d, layers)

    def other_row(d):
        return lax.rem(row + d, rows)

    def to(l, r):
        return {"layer": l, "row": r}

    def send(src, dst, send_sem, recv_sem, device):
        return pltpu.make_async_remote_copy(
            src_ref=src, dst_ref=dst, send_sem=send_sem, recv_sem=recv_sem,
            device_id=device, device_id_type=pl.DeviceIdType.MESH,
        )

    def here(dst, sem):
        send(dst, dst, sem, sem, to(layer, sibling)).wait_recv()

    def sent(src, sem):
        send(src, src, sem, sem, to(layer, sibling)).wait_send()

    def pl_piece(l, r):
        return plw.at[l, :, pl.ds(pl.multiple_of(r * piece, piece), piece)]

    def pr_piece(r):
        return prw.at[:, pl.ds(pl.multiple_of(r * piece, piece), piece)]

    def used(l):
        return min(width, -(-((l + 1) * rows * strip) // 128) * 128)

    def p_strip(l, r):
        start = pl.multiple_of((l * rows + r) * strip, strip)
        return pw.at[pl.ds(start, strip), pl.ds(0, used(l))]

    def sides(l, source=None):
        both = [side for side in (0, 1) if 0 <= l + 2 * side - 1 < layers]
        if source is None:
            return both
        return [side for side in both if side == (source < l)]

    def sources(l):
        return sorted((i for i in range(layers) if i != l), key=lambda i: (abs(i - l), i))

    def own_strip(l):
        return pf_ref.at[:, pl.ds(0, used(l))]

    barrier = pltpu.get_barrier_semaphore()
    for d in range(1, layers):
        pl.semaphore_signal(
            barrier, inc=1, device_id=to(other_layer(d), row), device_id_type=pl.DeviceIdType.MESH
        )
    for d in range(1, rows):
        pl.semaphore_signal(
            barrier, inc=1, device_id=to(layer, other_row(d)), device_id_type=pl.DeviceIdType.MESH
        )
    own_count, own_first = pick(count, layer), pick(first, layer)
    own_rows = pl.ds(pl.multiple_of((layer * rows + row) * strip, strip), strip)
    loads = [
        pltpu.make_async_copy(src, dst, load.at[i])
        for i, (src, dst) in enumerate([
            (pr_ref, pr_piece(row)), (pl_ref, pl_piece(layer, row)), (sk_ref, skv), (tr_ref, trv),
            (or_ref, orv.at[:, 0]), (or_ref, orv.at[:, 1]), (pf_ref, pw.at[own_rows, :]),
        ])
    ]
    for s in range(slots):
        t = own_first + jnp.minimum(s, own_count - 1)
        loads.append(pltpu.make_async_copy(ol_ref.at[t], zbuf.at[s, 0], local.at[0, s]))
        loads.append(pltpu.make_async_copy(tl_ref.at[t], zbuf.at[s, layer + 1], local.at[1, s]))
    for copy in loads:
        copy.start()
    pl.semaphore_wait(barrier, layers + rows - 2)

    for d in range(1, rows):
        send(pr_ref, pr_piece(row), pr_send.at[d], pr_recv.at[row], to(layer, other_row(d))).start()
        send(
            pl_ref, pl_piece(layer, row), pl_send.at[d], pl_recv.at[layer, row],
            to(layer, other_row(d)),
        ).start()
    for l in range(layers):

        @pl.when(layer == l)
        def _():
            for side in sides(l):
                send(
                    pl_ref, pl_piece(l, row), plz_send.at[l, side], pl_recv.at[l, row], to(l + 2 * side - 1, row)
                ).start()
                send(
                    own_strip(l), p_strip(l, row), pz_send.at[l, side], p_recv.at[l, row],
                    to(l + 2 * side - 1, row),
                ).start()
            for d in range(1, chips):
                send(
                    own_strip(l), p_strip(l, row), pf_send.at[l, d], p_recv.at[l, row],
                    to(layer, other_row(2 * d)),
                ).start()

    for l in range(layers):
        for s in range(count[l]):
            t = first[l] + s

            @pl.when(layer != l)
            def _():
                send(
                    tl_ref.at[t], zbuf.at[s, layer + 1], tl_send.at[t], tl_recv.at[s, layer], to(l, row)
                ).start()

    fbuf[...] = jnp.zeros_like(fbuf)
    eye = (
        lax.broadcasted_iota(jnp.int32, (rank, rank), 0) == lax.broadcasted_iota(jnp.int32, (rank, rank), 1)
    ).astype(F32)
    for copy in loads:
        copy.wait()
    for s in range(slots):
        t = own_first + jnp.minimum(s, own_count - 1)
        fbuf[s, 0:rank, 0:rank] = dot(orv[t, 0], skv[...], NT)
        fbuf[s, 0:rank, rank : 2 * rank] = eye

    for d in range(1, rows):
        here(pr_piece(other_row(d)), pr_recv.at[other_row(d)])
        here(pl_piece(layer, other_row(d)), pl_recv.at[layer, other_row(d)])
    coupling = dot(trv[...].reshape(tiles * rank, width), prw[...], NT)
    sketched = dot(plw[layer], skv[...], NT)
    chained = dot(coupling, sketched, NN, HIGHEST)
    for t in range(tiles):
        weight = -(mask_ref[t].astype(F32))
        block = slice(t * rank, (t + 1) * rank)
        ce[t, :, 0:rank] = chained[block] * weight
        ce[t, :, rank : 2 * rank] = coupling[block] * weight
    for l in range(layers):
        for s in range(count[l]):
            t = first[l] + s

            @pl.when(layer != l)
            def _():
                send(
                    ce.at[t], cebuf.at[s, layer], ce_send.at[t], ce_recv.at[s, layer], to(l, row)
                ).start()

            @pl.when(layer == l)
            def _():
                cebuf[s, layer] = ce[t]

    for me in range(layers):

        @pl.when(layer == me)
        def _():
            for l in sources(me):
                here(pl_piece(l, row), pl_recv.at[l, row])
                here(p_strip(l, row), p_recv.at[l, row])
                for side in sides(me, l):
                    send(
                        pl_piece(l, row), pl_piece(l, row), plz_send.at[l, side], pl_recv.at[l, row],
                        to(me + 2 * side - 1, row),
                    ).start()
                    send(
                        p_strip(l, row), p_strip(l, row), pz_send.at[l, side], p_recv.at[l, row],
                        to(me + 2 * side - 1, row),
                    ).start()
                for d in range(1, rows):
                    send(
                        pl_piece(l, row), pl_piece(l, row), plf_send.at[l, d], pl_recv.at[l, row],
                        to(layer, other_row(d)),
                    ).start()
                for d in range(1, chips):
                    send(
                        p_strip(l, row), p_strip(l, row), pf_send.at[l, d], p_recv.at[l, row],
                        to(layer, other_row(2 * d)),
                    ).start()

    for l in range(layers):

        @pl.when(layer == l)
        def _():
            for s in range(count[l]):
                for k in range(layers):
                    if k != l:
                        here(zbuf.at[s, k + 1], tl_recv.at[s, k])
                        here(cebuf.at[s, k], ce_recv.at[s, k])

    parts = []
    for s in range(slots):
        at = jnp.minimum(s, own_count - 1)
        z = zbuf[at].reshape((layers + 1) * rank, width)
        gram = dot(z, z, NT)
        for k in range(layers):
            block = slice((k + 1) * rank, (k + 2) * rank)
            fbuf[s, block, 0:rank] = cebuf[at, k, :, 0:rank]
            fbuf[s, block, (k + 2) * rank : (k + 3) * rank] = cebuf[at, k, :, rank : 2 * rank]
        joined = dot6(fbuf[s, :, 0:rank].T, gram)
        parts.append(dot6(joined, fbuf[s])[None])
    found = eliminate(jnp.concatenate(parts, axis=0), rank)
    for l in range(layers):

        @pl.when(layer == l)
        def _():
            for s in range(count[l]):
                t = first[l] + s
                high, low = split(found[s][:, rank:])
                mall[t, :, 0:rank] = high[:, 0:rank]
                mall[t, :, rank : 2 * rank] = low[:, 0:rank]
                mall[t, :, 2 * rank : (layers + 2) * rank] = high[:, rank:]
                mall[t, :, (layers + 2) * rank :] = low[:, rank:]
                for d in range(1, layers):
                    send(
                        mall.at[t], mall.at[t], m_send.at[t, d], m_recv.at[t], to(other_layer(d), row)
                    ).start()

    for d in range(chips):
        for l in range(layers):
            r = other_row(2 * d)
            if d:
                here(p_strip(l, r), p_recv.at[l, r])
            send(
                p_strip(l, r), p_strip(l, r), p3_send.at[l, d], p_recv.at[l, r], to(layer, sibling)
            ).start()

    for l in range(layers):
        for d in range(chips):
            r = lax.rem(sibling + 2 * d, rows)
            here(p_strip(l, r), p_recv.at[l, r])
    chunk = 256
    half = chunk // 2
    chunks = width // chunk
    inverses = invert_lower(
        [pw[i * half : (i + 1) * half, i * half : (i + 1) * half] for i in range(2 * chunks)], half
    )
    inner = [
        dot(pw[c * chunk + half : (c + 1) * chunk, c * chunk : c * chunk + half], inverses[2 * c], NN, HIGHEST)
        for c in range(chunks)
    ]
    for c in range(chunks):
        cross = dot(inverses[2 * c + 1], inner[c], NN, HIGHEST)
        for part, value in enumerate(split(inverses[2 * c])):
            diag[part, c, 0:half, 0:half] = value
        for part, value in enumerate(split(inverses[2 * c + 1])):
            diag[part, c, half:chunk, half:chunk] = value
        for part, value in enumerate(split(-cross)):
            diag[part, c, half:chunk, 0:half] = value
            diag[part, c, 0:half, half:chunk] = jnp.zeros_like(value)
        if c:
            rows_at = slice(c * chunk, (c + 1) * chunk)
            for part, value in enumerate(split(pw[rows_at, 0 : c * chunk])):
                below[part, rows_at, 0 : c * chunk] = value

    for l in range(layers):

        @pl.when(layer != l)
        def _():
            for d in range(1, rows):
                here(pl_piece(l, other_row(d)), pl_recv.at[l, other_row(d)])
            for s in range(count[l]):
                here(mall.at[first[l] + s], m_recv.at[first[l] + s])

    panels = plw[...].reshape(layers * rank, width)
    for t in range(tiles):
        core[t * rank : (t + 1) * rank, :] = dot(
            mall[t, :, 0 : 2 * rank], orv[t].reshape(2 * rank, width), NN
        )
    high = mall[:, :, 2 * rank : (layers + 2) * rank].reshape(tiles * rank, layers * rank)
    low = mall[:, :, (layers + 2) * rank :].reshape(tiles * rank, layers * rank)
    solved = []
    outs = []
    for c in range(chunks):
        cols = slice(c * chunk, (c + 1) * chunk)
        rest = core[:, cols] + (dot(high, panels[:, cols], NN) + dot(low, panels[:, cols], NN))
        for i in range(c):
            at = slice(i * chunk, (i + 1) * chunk)
            rest = rest - dot3(solved[i], (below[0, cols, at], below[1, cols, at]), NT)
        x = dot3(split(rest), (diag[0, c], diag[1, c]), NT)
        xv[:, :, cols] = x.reshape(tiles, rank, chunk)
        outs.append(
            pltpu.make_async_copy(
                xv.at[:, :, pl.ds(c * chunk, chunk)], out_ref.at[:, :, pl.ds(c * chunk, chunk)], leave.at[c]
            )
        )
        outs[-1].start()
        if c + 1 < chunks:
            solved.append(split(x))

    for copy in outs:
        copy.wait()
    for d in range(1, rows):
        sent(pr_piece(row), pr_send.at[d])
        sent(pl_piece(layer, row), pl_send.at[d])
    for l in range(layers):
        for d in range(1, chips):
            sent(p_strip(l, row), pf_send.at[l, d])
        for d in range(chips):
            sent(p_strip(l, other_row(2 * d)), p3_send.at[l, d])

        @pl.when(layer == l)
        def _():
            for side in sides(l):
                sent(pl_piece(l, row), plz_send.at[l, side])
                sent(p_strip(l, row), pz_send.at[l, side])
            for source in sources(l):
                for side in sides(l, source):
                    sent(pl_piece(source, row), plz_send.at[source, side])
                    sent(p_strip(source, row), pz_send.at[source, side])
            for d in range(1, layers):
                for s in range(count[l]):
                    sent(mall.at[first[l] + s], m_send.at[first[l] + s, d])

        @pl.when(layer != l)
        def _():
            for d in range(1, rows):
                sent(pl_piece(l, row), plf_send.at[l, d])
            for s in range(count[l]):
                sent(tl_ref.at[first[l] + s], tl_send.at[first[l] + s])
                sent(ce.at[first[l] + s], ce_send.at[first[l] + s])


def shards_kernel(layers, rows, tile_left, tile_right, tile_mask, orig_left, orig_right, pivot_left, pivot_right, sketch, pivot_factor):
    tiles, _, rank, width = tile_left.shape
    slots = max(owners(tiles, layers)[0])
    dma = pltpu.SemaphoreType.DMA
    hbm = pl.BlockSpec(memory_space=pltpu.HBM)
    lanes = (layers + 2) * rank
    return pl.pallas_call(
        partial(kernel, layers, rows),
        out_shape=jax.ShapeDtypeStruct((tiles, rank, width), F32),
        in_specs=[pl.BlockSpec(memory_space=pltpu.SMEM)] + [hbm] * 8,
        out_specs=hbm,
        scratch_shapes=[
            pltpu.VMEM((rank, width), BF16),
            pltpu.VMEM((layers, rank, width), BF16),
            pltpu.VMEM((width, width), F32),
            pltpu.VMEM((slots, layers + 1, rank, width), BF16),
            pltpu.VMEM((tiles, rank, 2 * rank), F32),
            pltpu.VMEM((slots, layers, rank, 2 * rank), F32),
            pltpu.VMEM((slots, (layers + 1) * rank, lanes), F32),
            pltpu.VMEM((tiles, rank, 2 * (layers + 1) * rank), BF16),
            pltpu.VMEM((2, width // 256, 256, 256), BF16),
            pltpu.VMEM((2, width, width), BF16),
            pltpu.VMEM((tiles * rank, width), F32),
            pltpu.VMEM((tiles, rank, width), BF16),
            pltpu.VMEM((tiles, 2, rank, width), BF16),
            pltpu.VMEM((rank, width), BF16),
            pltpu.VMEM((tiles, rank, width), F32),
            dma((rows,)), dma((rows,)), dma((rows,)), dma((layers, rows)),
            dma((layers, 2)), dma((layers, rows)), dma((layers, rows)), dma((layers, rows)),
            dma((layers, 2)), dma((layers, rows)),
            dma((tiles,)), dma((slots, layers)), dma((tiles,)), dma((slots, layers)),
            dma((tiles, layers)), dma((tiles,)), dma((7,)), dma((2, slots)), dma((width // 256,)),
        ],
        compiler_params=pltpu.CompilerParams(
            collective_id=0, has_side_effects=True, vmem_limit_bytes=63 * 1024 * 1024
        ),
    )(
        tile_mask.reshape(tiles), tile_left.reshape(tiles, rank, width), tile_right.reshape(tiles, rank, width),
        orig_left, orig_right, pivot_left.reshape(rank, -1), pivot_right.reshape(rank, -1),
        sketch, pivot_factor,
    )


def shards_general(
    tile_left,
    tile_right,
    tile_mask,
    orig_left,
    orig_right,
    pivot_left,
    pivot_right,
    sketch,
    pivot_factor,
):
    highest = HIGHEST
    pivot_whole = lax.all_gather(pivot_factor, ("layer", "row"), axis=0, tiled=True)
    left_whole, right_whole = (
        lax.all_gather(pivot_left, "row", axis=2, tiled=True),
        lax.all_gather(pivot_right, "row", axis=2, tiled=True),
    )
    coupling = jnp.einsum("tpqb,psb->tpqs", tile_right, right_whole, preferred_element_type=F32)
    weights = tile_mask.astype(F32)[:, :, None, None]
    update_left = jnp.einsum("tpqs,tpqb->tpsb", coupling, tile_left.astype(F32), precision=highest) * weights
    sketched = jnp.einsum("pqb,sb->pqs", left_whole, sketch, preferred_element_type=F32)
    partial_sample = jnp.einsum("tpqb,pqs->tsb", update_left, sketched, precision=highest)
    orig_float = orig_left.astype(F32)
    orig_sketch = jnp.einsum("tqb,sb->tqs", orig_right, sketch, preferred_element_type=F32)
    own_sample = jnp.einsum("tqb,tqs->tsb", orig_float, orig_sketch, precision=highest)
    sample = own_sample - lax.psum(partial_sample, "layer")
    gram_matrix = jnp.einsum("tqb,tsb->tqs", sample, sample, precision=highest)
    factor = jnp.linalg.cholesky(gram_matrix)
    row_basis = jax.vmap(partial(jax.scipy.linalg.solve_triangular, lower=True))(factor, sample)
    projected = jnp.einsum("tpqb,tsb->tpqs", update_left, row_basis, precision=highest)
    partial_core = jnp.einsum("pqb,tpqs->tsb", left_whole.astype(F32), projected, precision=highest)
    orig_basis = jnp.einsum("tqb,tsb->tqs", orig_float, row_basis, precision=highest)
    own_core = jnp.einsum("tqb,tqs->tsb", orig_right.astype(F32), orig_basis, precision=highest)
    core = own_core - lax.psum(partial_core, "layer")
    tile_count, rank_rows, cell_count = core.shape
    right_sides = core.reshape(tile_count * rank_rows, cell_count).T
    solution = jax.scipy.linalg.solve_triangular(pivot_whole, right_sides, lower=True)
    return solution.T.reshape(tile_count, rank_rows, cell_count)


def solution(mesh):
    in_specs = (
        P("row", "layer", None, None),
        P("row", "layer", None, None),
        P("row", "layer"),
        P("row", None, None),
        P("row", None, None),
        P("layer", None, "row"),
        P("layer", None, "row"),
        P(),
        P(("layer", "row"), None),
    )
    out_specs = P("row", None, None)
    layers, rows = mesh.shape["layer"], mesh.shape["row"]

    def shards(*blocks):
        tiles, panels, rank, width = blocks[0].shape
        fits = (
            panels == 1 and tiles >= layers and rank == 64 and width % 256 == 0 and rows % 2 == 0
            and width % (128 * rows) == 0 and width % (8 * layers * rows) == 0
        )
        if fits:
            return shards_kernel(layers, rows, *blocks)
        return shards_general(*blocks)

    return jax.shard_map(shards, mesh=mesh, in_specs=in_specs, out_specs=out_specs, check_vma=False)
```

```python
from functools import partial

import jax
import jax.numpy as jnp
from jax import lax
from jax.experimental import pallas as pl
from jax.experimental.pallas import tpu as pltpu
from jax.sharding import PartitionSpec as P

HIGHEST = lax.Precision.HIGHEST
F32 = jnp.float32
BF16 = jnp.bfloat16
NN = (((1,), (0,)), ((), ()))
NT = (((1,), (1,)), ((), ()))


def dot(a, b, dims, precision=None):
    return lax.dot_general(a, b, dims, precision=precision, preferred_element_type=F32)


def split(x):
    high = x.astype(BF16)
    return high, (x - high.astype(F32)).astype(BF16)


def dot3(a, b, dims):
    (ah, al), (bh, bl) = a, b
    return dot(ah, bh, dims) + (dot(ah, bl, dims) + dot(al, bh, dims))


def split3(x):
    high = x.astype(BF16)
    rest = x - high.astype(F32)
    middle = rest.astype(BF16)
    return high, middle, (rest - middle.astype(F32)).astype(BF16)


def dot6(a, b):
    rows = a.shape[0]
    stacked = jnp.concatenate(split3(a), axis=0)
    high, middle, low = split3(b)
    by_high = dot(stacked, high, NN)
    by_middle = dot(stacked[: 2 * rows], middle, NN)
    by_low = dot(stacked[:rows], low, NN)
    small = by_high[2 * rows :] + by_middle[rows:] + by_low
    return by_high[:rows] + (by_high[rows : 2 * rows] + by_middle[:rows] + small)


def owners(tiles, layers):
    base, extra = divmod(tiles, layers)
    order = sorted(range(layers), key=lambda i: abs(2 * i - layers + 1))
    count = [base + (order.index(i) < extra) for i in range(layers)]
    first = [sum(count[:i]) for i in range(layers)]
    return count, first


def pick(table, index):
    value = jnp.int32(table[0])
    for i in range(1, len(table)):
        value = jnp.where(index == i, jnp.int32(table[i]), value)
    return value


def invert_lower(blocks, size):
    rows = lax.broadcasted_iota(jnp.int32, (size, size), 0)
    cols = lax.broadcasted_iota(jnp.int32, (size, size), 1)
    eye = rows == cols
    inverses = [jnp.where(eye, 1.0 / jnp.where(eye, block, 1.0), 0.0) for block in blocks]
    step = 1
    while step < size:
        pair = (rows // (2 * step) == cols // (2 * step)) & (rows // step > cols // step)
        inner = [
            dot(jnp.where(pair, block, 0.0), inverse, NN, HIGHEST) for block, inverse in zip(blocks, inverses)
        ]
        outer = [dot(inverse, right, NN, HIGHEST) for inverse, right in zip(inverses, inner)]
        inverses = [inverse - change for inverse, change in zip(inverses, outer)]
        step *= 2
    return inverses


def eliminate(augmented, rank):
    lanes = 128
    tiles = [augmented[:, :, i : i + lanes] for i in range(0, augmented.shape[2], lanes)]
    done = [[] for _ in tiles]
    roots = []
    for block in range(rank // 8):
        shape = tiles[0].shape
        index = lax.broadcasted_iota(jnp.int32, shape, 1)
        columns = [
            jnp.broadcast_to(tiles[0][:, :, block * 8 + at : block * 8 + at + 1], shape) for at in range(8)
        ]
        for at in range(8):
            pivot = columns[at][:, at : at + 1, :]
            weight = jnp.where(index > at, columns[at] * (1.0 / pivot), 0.0)
            for later in range(at + 1, 8):
                columns[later] = columns[later] - weight * columns[later][:, at : at + 1, :]
            tiles = [tile - weight * tile[:, at : at + 1, :] for tile in tiles]
            roots.append(lax.rsqrt(pivot))
        for i, tile in enumerate(tiles):
            done[i].append(tile[:, :8, :])
        tiles = [tile[:, 8:, :] for tile in tiles]
    scale = jnp.concatenate(roots, axis=1)
    return jnp.concatenate([jnp.concatenate(part, axis=1) * scale for part in done], axis=2)


def kernel(
    layers, rows, mask_ref, tl_ref, tr_ref, ol_ref, or_ref, pl_ref, pr_ref, sk_ref, pf_ref,
    out_ref,
    prw, plw, pw, zbuf, ce, cebuf, fbuf, mall, diag, below, core, trv, orv, skv, xv,
    pr_send, pr_recv, pl_send, pl_recv, pz_send, pf_send, p3_send, p_recv,
    plz_send, plf_send, tl_send, tl_recv, ce_send, ce_recv, m_send, m_recv, load, local, leave,
):
    layer, row = lax.axis_index("layer"), lax.axis_index("row")
    tiles, rank, width = tl_ref.shape
    piece = pl_ref.shape[1]
    strip = pf_ref.shape[0]
    count, first = owners(tiles, layers)
    slots = max(count)
    chips = rows // 2
    sibling = row + 1 - 2 * lax.rem(row, 2)

    def other_layer(d):
        return lax.rem(layer + d, layers)

    def other_row(d):
        return lax.rem(row + d, rows)

    def to(l, r):
        return {"layer": l, "row": r}

    def send(src, dst, send_sem, recv_sem, device):
        return pltpu.make_async_remote_copy(
            src_ref=src, dst_ref=dst, send_sem=send_sem, recv_sem=recv_sem,
            device_id=device, device_id_type=pl.DeviceIdType.MESH,
        )

    def here(dst, sem):
        send(dst, dst, sem, sem, to(layer, sibling)).wait_recv()

    def sent(src, sem):
        send(src, src, sem, sem, to(layer, sibling)).wait_send()

    def pl_piece(l, r):
        return plw.at[l, :, pl.ds(pl.multiple_of(r * piece, piece), piece)]

    def pr_piece(r):
        return prw.at[:, pl.ds(pl.multiple_of(r * piece, piece), piece)]

    def used(l):
        return min(width, -(-((l + 1) * rows * strip) // 128) * 128)

    def p_strip(l, r):
        start = pl.multiple_of((l * rows + r) * strip, strip)
        return pw.at[pl.ds(start, strip), pl.ds(0, used(l))]

    def sources(l):
        return sorted((i for i in range(layers) if i != l), key=lambda i: (abs(i - l), i))

    def own_strip(l):
        return pf_ref.at[:, pl.ds(0, used(l))]

    def share_strips(l):
        for d in range(chips):
            r = other_row(2 * d)
            if d:
                here(p_strip(l, r), p_recv.at[l, r])
            send(
                p_strip(l, r), p_strip(l, r), p3_send.at[l, d], p_recv.at[l, r], to(layer, sibling)
            ).start()

    barrier = pltpu.get_barrier_semaphore()
    for d in range(1, layers):
        pl.semaphore_signal(
            barrier, inc=1, device_id=to(other_layer(d), row), device_id_type=pl.DeviceIdType.MESH
        )
    for d in range(1, rows):
        pl.semaphore_signal(
            barrier, inc=1, device_id=to(layer, other_row(d)), device_id_type=pl.DeviceIdType.MESH
        )
    own_count, own_first = pick(count, layer), pick(first, layer)
    own_rows = pl.ds(pl.multiple_of((layer * rows + row) * strip, strip), strip)
    loads = [
        pltpu.make_async_copy(src, dst, load.at[i])
        for i, (src, dst) in enumerate([
            (pr_ref, pr_piece(row)), (pl_ref, pl_piece(layer, row)), (sk_ref, skv), (tr_ref, trv),
            (or_ref, orv.at[:, 0]), (or_ref, orv.at[:, 1]), (pf_ref, pw.at[own_rows, :]),
        ])
    ]
    for s in range(slots):
        t = own_first + jnp.minimum(s, own_count - 1)
        loads.append(pltpu.make_async_copy(ol_ref.at[t], zbuf.at[s, 0], local.at[0, s]))
        loads.append(pltpu.make_async_copy(tl_ref.at[t], zbuf.at[s, layer + 1], local.at[1, s]))
    for copy in loads:
        copy.start()
    pl.semaphore_wait(barrier, layers + rows - 2)

    for d in range(1, rows):
        send(pr_ref, pr_piece(row), pr_send.at[d], pr_recv.at[row], to(layer, other_row(d))).start()
        send(
            pl_ref, pl_piece(layer, row), pl_send.at[d], pl_recv.at[layer, row],
            to(layer, other_row(d)),
        ).start()
    for d in range(1, layers):
        send(
            pl_ref, pl_piece(layer, row), plz_send.at[d], pl_recv.at[layer, row], to(other_layer(d), row)
        ).start()
    for l in range(layers):

        @pl.when(layer == l)
        def _():
            for d in range(1, chips):
                send(
                    own_strip(l), p_strip(l, row), pf_send.at[l, d], p_recv.at[l, row],
                    to(layer, other_row(2 * d)),
                ).start()

    for l in range(layers):
        for s in range(count[l]):
            t = first[l] + s

            @pl.when(layer != l)
            def _():
                send(
                    tl_ref.at[t], zbuf.at[s, layer + 1], tl_send.at[t], tl_recv.at[s, layer], to(l, row)
                ).start()

    fbuf[...] = jnp.zeros_like(fbuf)
    eye = (
        lax.broadcasted_iota(jnp.int32, (rank, rank), 0) == lax.broadcasted_iota(jnp.int32, (rank, rank), 1)
    ).astype(F32)
    for copy in loads:
        copy.wait()
    for s in range(slots):
        t = own_first + jnp.minimum(s, own_count - 1)
        fbuf[s, 0:rank, 0:rank] = dot(orv[t, 0], skv[...], NT)
        fbuf[s, 0:rank, rank : 2 * rank] = eye

    for d in range(1, rows):
        here(pr_piece(other_row(d)), pr_recv.at[other_row(d)])
        here(pl_piece(layer, other_row(d)), pl_recv.at[layer, other_row(d)])
    coupling = dot(trv[...].reshape(tiles * rank, width), prw[...], NT)
    sketched = dot(plw[layer], skv[...], NT)
    chained = dot(coupling, sketched, NN, HIGHEST)
    for t in range(tiles):
        weight = -(mask_ref[t].astype(F32))
        block = slice(t * rank, (t + 1) * rank)
        ce[t, :, 0:rank] = chained[block] * weight
        ce[t, :, rank : 2 * rank] = coupling[block] * weight
    for l in range(layers):
        for s in range(count[l]):
            t = first[l] + s

            @pl.when(layer != l)
            def _():
                send(
                    ce.at[t], cebuf.at[s, layer], ce_send.at[t], ce_recv.at[s, layer], to(l, row)
                ).start()

            @pl.when(layer == l)
            def _():
                cebuf[s, layer] = ce[t]

    for me in range(layers):

        @pl.when(layer == me)
        def _():
            for l in sources(me):
                here(pl_piece(l, row), pl_recv.at[l, row])
                for d in range(1, rows):
                    send(
                        pl_piece(l, row), pl_piece(l, row), plf_send.at[l, d], pl_recv.at[l, row],
                        to(layer, other_row(d)),
                    ).start()
            share_strips(me)
            for l in range(layers):
                for s in range(count[l] if l != me else 0):
                    sent(tl_ref.at[first[l] + s], tl_send.at[first[l] + s])
            for l in reversed(sources(me)):
                send(
                    own_strip(me), p_strip(me, row), pz_send.at[l], p_recv.at[me, row], to(l, row)
                ).start()

    for l in range(layers):

        @pl.when(layer == l)
        def _():
            for s in range(count[l]):
                for k in range(layers):
                    if k != l:
                        here(zbuf.at[s, k + 1], tl_recv.at[s, k])
                        here(cebuf.at[s, k], ce_recv.at[s, k])

    parts = []
    for s in range(slots):
        at = jnp.minimum(s, own_count - 1)
        z = zbuf[at].reshape((layers + 1) * rank, width)
        gram = dot(z, z, NT)
        for k in range(layers):
            block = slice((k + 1) * rank, (k + 2) * rank)
            fbuf[s, block, 0:rank] = cebuf[at, k, :, 0:rank]
            fbuf[s, block, (k + 2) * rank : (k + 3) * rank] = cebuf[at, k, :, rank : 2 * rank]
        joined = dot6(fbuf[s, :, 0:rank].T, gram)
        parts.append(dot6(joined, fbuf[s])[None])
    found = eliminate(jnp.concatenate(parts, axis=0), rank)
    for l in range(layers):

        @pl.when(layer == l)
        def _():
            for s in range(count[l]):
                t = first[l] + s
                high, low = split(found[s][:, rank:])
                mall[t, :, 0:rank] = high[:, 0:rank]
                mall[t, :, rank : 2 * rank] = low[:, 0:rank]
                mall[t, :, 2 * rank : (layers + 2) * rank] = high[:, rank:]
                mall[t, :, (layers + 2) * rank :] = low[:, rank:]
                for d in range(1, layers):
                    send(
                        mall.at[t], mall.at[t], m_send.at[t, d], m_recv.at[t], to(other_layer(d), row)
                    ).start()

    for me in range(layers):

        @pl.when(layer == me)
        def _():
            for l in sources(me):
                here(p_strip(l, row), p_recv.at[l, row])
                for d in range(1, chips):
                    send(
                        p_strip(l, row), p_strip(l, row), pf_send.at[l, d], p_recv.at[l, row],
                        to(layer, other_row(2 * d)),
                    ).start()
            for l in sources(me):
                share_strips(l)

    for l in range(layers):
        for d in range(chips):
            r = lax.rem(sibling + 2 * d, rows)
            here(p_strip(l, r), p_recv.at[l, r])
    chunk = 256
    half = chunk // 2
    chunks = width // chunk
    inverses = invert_lower(
        [pw[i * half : (i + 1) * half, i * half : (i + 1) * half] for i in range(2 * chunks)], half
    )
    inner = [
        dot(pw[c * chunk + half : (c + 1) * chunk, c * chunk : c * chunk + half], inverses[2 * c], NN, HIGHEST)
        for c in range(chunks)
    ]
    for c in range(chunks):
        cross = dot(inverses[2 * c + 1], inner[c], NN, HIGHEST)
        for part, value in enumerate(split(inverses[2 * c])):
            diag[part, c, 0:half, 0:half] = value
        for part, value in enumerate(split(inverses[2 * c + 1])):
            diag[part, c, half:chunk, half:chunk] = value
        for part, value in enumerate(split(-cross)):
            diag[part, c, half:chunk, 0:half] = value
            diag[part, c, 0:half, half:chunk] = jnp.zeros_like(value)
        if c:
            rows_at = slice(c * chunk, (c + 1) * chunk)
            for part, value in enumerate(split(pw[rows_at, 0 : c * chunk])):
                below[part, rows_at, 0 : c * chunk] = value

    for l in range(layers):

        @pl.when(layer != l)
        def _():
            for d in range(1, rows):
                here(pl_piece(l, other_row(d)), pl_recv.at[l, other_row(d)])
            for s in range(count[l]):
                here(mall.at[first[l] + s], m_recv.at[first[l] + s])

    panels = plw[...].reshape(layers * rank, width)
    for t in range(tiles):
        core[t * rank : (t + 1) * rank, :] = dot(
            mall[t, :, 0 : 2 * rank], orv[t].reshape(2 * rank, width), NN
        )
    high = mall[:, :, 2 * rank : (layers + 2) * rank].reshape(tiles * rank, layers * rank)
    low = mall[:, :, (layers + 2) * rank :].reshape(tiles * rank, layers * rank)
    solved = []
    outs = []
    for c in range(chunks):
        cols = slice(c * chunk, (c + 1) * chunk)
        rest = core[:, cols] + (dot(high, panels[:, cols], NN) + dot(low, panels[:, cols], NN))
        for i in range(c):
            at = slice(i * chunk, (i + 1) * chunk)
            rest = rest - dot3(solved[i], (below[0, cols, at], below[1, cols, at]), NT)
        x = dot3(split(rest), (diag[0, c], diag[1, c]), NT)
        xv[:, :, cols] = x.reshape(tiles, rank, chunk)
        outs.append(
            pltpu.make_async_copy(
                xv.at[:, :, pl.ds(c * chunk, chunk)], out_ref.at[:, :, pl.ds(c * chunk, chunk)], leave.at[c]
            )
        )
        outs[-1].start()
        if c + 1 < chunks:
            solved.append(split(x))

    for copy in outs:
        copy.wait()
    for d in range(1, rows):
        sent(pr_piece(row), pr_send.at[d])
        sent(pl_piece(layer, row), pl_send.at[d])
    for d in range(1, layers):
        sent(pl_piece(layer, row), plz_send.at[d])
    for l in range(layers):
        for d in range(1, chips):
            sent(p_strip(l, row), pf_send.at[l, d])
        for d in range(chips):
            sent(p_strip(l, other_row(2 * d)), p3_send.at[l, d])

        @pl.when(layer == l)
        def _():
            for other in sources(l):
                sent(p_strip(l, row), pz_send.at[other])
            for d in range(1, layers):
                for s in range(count[l]):
                    sent(mall.at[first[l] + s], m_send.at[first[l] + s, d])

        @pl.when(layer != l)
        def _():
            for d in range(1, rows):
                sent(pl_piece(l, row), plf_send.at[l, d])
            for s in range(count[l]):
                sent(ce.at[first[l] + s], ce_send.at[first[l] + s])


def shards_kernel(layers, rows, tile_left, tile_right, tile_mask, orig_left, orig_right, pivot_left, pivot_right, sketch, pivot_factor):
    tiles, _, rank, width = tile_left.shape
    slots = max(owners(tiles, layers)[0])
    dma = pltpu.SemaphoreType.DMA
    hbm = pl.BlockSpec(memory_space=pltpu.HBM)
    lanes = (layers + 2) * rank
    return pl.pallas_call(
        partial(kernel, layers, rows),
        out_shape=jax.ShapeDtypeStruct((tiles, rank, width), F32),
        in_specs=[pl.BlockSpec(memory_space=pltpu.SMEM)] + [hbm] * 8,
        out_specs=hbm,
        scratch_shapes=[
            pltpu.VMEM((rank, width), BF16),
            pltpu.VMEM((layers, rank, width), BF16),
            pltpu.VMEM((width, width), F32),
            pltpu.VMEM((slots, layers + 1, rank, width), BF16),
            pltpu.VMEM((tiles, rank, 2 * rank), F32),
            pltpu.VMEM((slots, layers, rank, 2 * rank), F32),
            pltpu.VMEM((slots, (layers + 1) * rank, lanes), F32),
            pltpu.VMEM((tiles, rank, 2 * (layers + 1) * rank), BF16),
            pltpu.VMEM((2, width // 256, 256, 256), BF16),
            pltpu.VMEM((2, width, width), BF16),
            pltpu.VMEM((tiles * rank, width), F32),
            pltpu.VMEM((tiles, rank, width), BF16),
            pltpu.VMEM((tiles, 2, rank, width), BF16),
            pltpu.VMEM((rank, width), BF16),
            pltpu.VMEM((tiles, rank, width), F32),
            dma((rows,)), dma((rows,)), dma((rows,)), dma((layers, rows)),
            dma((layers,)), dma((layers, rows)), dma((layers, rows)), dma((layers, rows)),
            dma((layers,)), dma((layers, rows)),
            dma((tiles,)), dma((slots, layers)), dma((tiles,)), dma((slots, layers)),
            dma((tiles, layers)), dma((tiles,)), dma((7,)), dma((2, slots)), dma((width // 256,)),
        ],
        compiler_params=pltpu.CompilerParams(
            collective_id=0, has_side_effects=True, vmem_limit_bytes=63 * 1024 * 1024
        ),
    )(
        tile_mask.reshape(tiles), tile_left.reshape(tiles, rank, width), tile_right.reshape(tiles, rank, width),
        orig_left, orig_right, pivot_left.reshape(rank, -1), pivot_right.reshape(rank, -1),
        sketch, pivot_factor,
    )


def shards_general(
    tile_left,
    tile_right,
    tile_mask,
    orig_left,
    orig_right,
    pivot_left,
    pivot_right,
    sketch,
    pivot_factor,
):
    highest = HIGHEST
    pivot_whole = lax.all_gather(pivot_factor, ("layer", "row"), axis=0, tiled=True)
    left_whole, right_whole = (
        lax.all_gather(pivot_left, "row", axis=2, tiled=True),
        lax.all_gather(pivot_right, "row", axis=2, tiled=True),
    )
    coupling = jnp.einsum("tpqb,psb->tpqs", tile_right, right_whole, preferred_element_type=F32)
    weights = tile_mask.astype(F32)[:, :, None, None]
    update_left = jnp.einsum("tpqs,tpqb->tpsb", coupling, tile_left.astype(F32), precision=highest) * weights
    sketched = jnp.einsum("pqb,sb->pqs", left_whole, sketch, preferred_element_type=F32)
    partial_sample = jnp.einsum("tpqb,pqs->tsb", update_left, sketched, precision=highest)
    orig_float = orig_left.astype(F32)
    orig_sketch = jnp.einsum("tqb,sb->tqs", orig_right, sketch, preferred_element_type=F32)
    own_sample = jnp.einsum("tqb,tqs->tsb", orig_float, orig_sketch, precision=highest)
    sample = own_sample - lax.psum(partial_sample, "layer")
    gram_matrix = jnp.einsum("tqb,tsb->tqs", sample, sample, precision=highest)
    factor = jnp.linalg.cholesky(gram_matrix)
    row_basis = jax.vmap(partial(jax.scipy.linalg.solve_triangular, lower=True))(factor, sample)
    projected = jnp.einsum("tpqb,tsb->tpqs", update_left, row_basis, precision=highest)
    partial_core = jnp.einsum("pqb,tpqs->tsb", left_whole.astype(F32), projected, precision=highest)
    orig_basis = jnp.einsum("tqb,tsb->tqs", orig_float, row_basis, precision=highest)
    own_core = jnp.einsum("tqb,tqs->tsb", orig_right.astype(F32), orig_basis, precision=highest)
    core = own_core - lax.psum(partial_core, "layer")
    tile_count, rank_rows, cell_count = core.shape
    right_sides = core.reshape(tile_count * rank_rows, cell_count).T
    solution = jax.scipy.linalg.solve_triangular(pivot_whole, right_sides, lower=True)
    return solution.T.reshape(tile_count, rank_rows, cell_count)


def solution(mesh):
    in_specs = (
        P("row", "layer", None, None),
        P("row", "layer", None, None),
        P("row", "layer"),
        P("row", None, None),
        P("row", None, None),
        P("layer", None, "row"),
        P("layer", None, "row"),
        P(),
        P(("layer", "row"), None),
    )
    out_specs = P("row", None, None)
    layers, rows = mesh.shape["layer"], mesh.shape["row"]

    def shards(*blocks):
        tiles, panels, rank, width = blocks[0].shape
        fits = (
            panels == 1 and tiles >= layers and rank == 64 and width % 256 == 0 and rows % 2 == 0
            and width % (128 * rows) == 0 and width % (8 * layers * rows) == 0
        )
        if fits:
            return shards_kernel(layers, rows, *blocks)
        return shards_general(*blocks)

    return jax.shard_map(shards, mesh=mesh, in_specs=in_specs, out_specs=out_specs, check_vma=False)
```

```python
from functools import partial

import jax
import jax.numpy as jnp
from jax import lax
from jax.experimental import pallas as pl
from jax.experimental.pallas import tpu as pltpu
from jax.sharding import PartitionSpec as P

HIGHEST = lax.Precision.HIGHEST
F32 = jnp.float32
BF16 = jnp.bfloat16
NN = (((1,), (0,)), ((), ()))
NT = (((1,), (1,)), ((), ()))


def dot(a, b, dims, precision=None):
    return lax.dot_general(a, b, dims, precision=precision, preferred_element_type=F32)


def split(x):
    high = x.astype(BF16)
    return high, (x - high.astype(F32)).astype(BF16)


def dot3(a, b, dims):
    (ah, al), (bh, bl) = a, b
    return dot(ah, bh, dims) + (dot(ah, bl, dims) + dot(al, bh, dims))


def split3(x):
    high = x.astype(BF16)
    rest = x - high.astype(F32)
    middle = rest.astype(BF16)
    return high, middle, (rest - middle.astype(F32)).astype(BF16)


def dot6(a, b):
    rows = a.shape[0]
    stacked = jnp.concatenate(split3(a), axis=0)
    high, middle, low = split3(b)
    by_high = dot(stacked, high, NN)
    by_middle = dot(stacked[: 2 * rows], middle, NN)
    by_low = dot(stacked[:rows], low, NN)
    small = by_high[2 * rows :] + by_middle[rows:] + by_low
    return by_high[:rows] + (by_high[rows : 2 * rows] + by_middle[:rows] + small)


def owners(tiles, layers):
    base, extra = divmod(tiles, layers)
    order = sorted(range(layers), key=lambda i: abs(2 * i - layers + 1))
    count = [base + (order.index(i) < extra) for i in range(layers)]
    first = [sum(count[:i]) for i in range(layers)]
    return count, first


def pick(table, index):
    value = jnp.int32(table[0])
    for i in range(1, len(table)):
        value = jnp.where(index == i, jnp.int32(table[i]), value)
    return value


def invert_lower(blocks, size):
    rows = lax.broadcasted_iota(jnp.int32, (size, size), 0)
    cols = lax.broadcasted_iota(jnp.int32, (size, size), 1)
    eye = rows == cols
    inverses = [jnp.where(eye, 1.0 / jnp.where(eye, block, 1.0), 0.0) for block in blocks]
    step = 1
    while step < size:
        pair = (rows // (2 * step) == cols // (2 * step)) & (rows // step > cols // step)
        inner = [
            dot(jnp.where(pair, block, 0.0), inverse, NN, HIGHEST) for block, inverse in zip(blocks, inverses)
        ]
        outer = [dot(inverse, right, NN, HIGHEST) for inverse, right in zip(inverses, inner)]
        inverses = [inverse - change for inverse, change in zip(inverses, outer)]
        step *= 2
    return inverses


def eliminate(augmented, rank):
    lanes = 128
    tiles = [augmented[:, :, i : i + lanes] for i in range(0, augmented.shape[2], lanes)]
    done = [[] for _ in tiles]
    roots = []
    for block in range(rank // 8):
        shape = tiles[0].shape
        index = lax.broadcasted_iota(jnp.int32, shape, 1)
        columns = [
            jnp.broadcast_to(tiles[0][:, :, block * 8 + at : block * 8 + at + 1], shape) for at in range(8)
        ]
        for at in range(8):
            pivot = columns[at][:, at : at + 1, :]
            weight = jnp.where(index > at, columns[at] * (1.0 / pivot), 0.0)
            for later in range(at + 1, 8):
                columns[later] = columns[later] - weight * columns[later][:, at : at + 1, :]
            tiles = [tile - weight * tile[:, at : at + 1, :] for tile in tiles]
            roots.append(lax.rsqrt(pivot))
        for i, tile in enumerate(tiles):
            done[i].append(tile[:, :8, :])
        tiles = [tile[:, 8:, :] for tile in tiles]
    scale = jnp.concatenate(roots, axis=1)
    return jnp.concatenate([jnp.concatenate(part, axis=1) * scale for part in done], axis=2)


def kernel(
    layers, rows, mask_ref, tl_ref, tr_ref, ol_ref, or_ref, pl_ref, pr_ref, sk_ref, pf_ref,
    out_ref,
    prw, plw, pw, zbuf, ce, cebuf, fbuf, mall, diag, below, core, trv, orv, skv, xv,
    pr_send, pr_recv, pl_send, pl_recv, pz_send, pf_send, p3_send, p_recv,
    plz_send, plf_send, tl_send, tl_recv, ce_send, ce_recv, m_send, m_recv, load, local, leave,
):
    layer, row = lax.axis_index("layer"), lax.axis_index("row")
    tiles, rank, width = tl_ref.shape
    piece = pl_ref.shape[1]
    strip = pf_ref.shape[0]
    count, first = owners(tiles, layers)
    slots = max(count)
    chips = rows // 2
    sibling = row + 1 - 2 * lax.rem(row, 2)

    def other_layer(d):
        return lax.rem(layer + d, layers)

    def other_row(d):
        return lax.rem(row + d, rows)

    def to(l, r):
        return {"layer": l, "row": r}

    def send(src, dst, send_sem, recv_sem, device):
        return pltpu.make_async_remote_copy(
            src_ref=src, dst_ref=dst, send_sem=send_sem, recv_sem=recv_sem,
            device_id=device, device_id_type=pl.DeviceIdType.MESH,
        )

    def here(dst, sem):
        send(dst, dst, sem, sem, to(layer, sibling)).wait_recv()

    def sent(src, sem):
        send(src, src, sem, sem, to(layer, sibling)).wait_send()

    def pl_piece(l, r):
        return plw.at[l, :, pl.ds(pl.multiple_of(r * piece, piece), piece)]

    def pr_piece(r):
        return prw.at[:, pl.ds(pl.multiple_of(r * piece, piece), piece)]

    def used(l):
        return min(width, -(-((l + 1) * rows * strip) // 128) * 128)

    def p_strip(l, r):
        start = pl.multiple_of((l * rows + r) * strip, strip)
        return pw.at[pl.ds(start, strip), pl.ds(0, used(l))]

    def sources(l):
        return sorted((i for i in range(layers) if i != l), key=lambda i: (abs(i - l), i))

    def own_strip(l):
        return pf_ref.at[:, pl.ds(0, used(l))]

    def share_strips(l):
        for d in range(chips):
            r = other_row(2 * d)
            if d:
                here(p_strip(l, r), p_recv.at[l, r])
            send(
                p_strip(l, r), p_strip(l, r), p3_send.at[l, d], p_recv.at[l, r], to(layer, sibling)
            ).start()

    barrier = pltpu.get_barrier_semaphore()
    for d in range(1, layers):
        pl.semaphore_signal(
            barrier, inc=1, device_id=to(other_layer(d), row), device_id_type=pl.DeviceIdType.MESH
        )
    for d in range(1, rows):
        pl.semaphore_signal(
            barrier, inc=1, device_id=to(layer, other_row(d)), device_id_type=pl.DeviceIdType.MESH
        )
    own_count, own_first = pick(count, layer), pick(first, layer)
    own_rows = pl.ds(pl.multiple_of((layer * rows + row) * strip, strip), strip)
    loads = [
        pltpu.make_async_copy(src, dst, load.at[i])
        for i, (src, dst) in enumerate([
            (pr_ref, pr_piece(row)), (pl_ref, pl_piece(layer, row)), (sk_ref, skv), (tr_ref, trv),
            (or_ref, orv.at[:, 0]), (or_ref, orv.at[:, 1]), (pf_ref, pw.at[own_rows, :]),
        ])
    ]
    for s in range(slots):
        t = own_first + jnp.minimum(s, own_count - 1)
        loads.append(pltpu.make_async_copy(ol_ref.at[t], zbuf.at[s, 0], local.at[0, s]))
        loads.append(pltpu.make_async_copy(tl_ref.at[t], zbuf.at[s, layer + 1], local.at[1, s]))
    for copy in loads:
        copy.start()
    pl.semaphore_wait(barrier, layers + rows - 2)

    for d in range(1, rows):
        send(pr_ref, pr_piece(row), pr_send.at[d], pr_recv.at[row], to(layer, other_row(d))).start()
        send(
            pl_ref, pl_piece(layer, row), pl_send.at[d], pl_recv.at[layer, row],
            to(layer, other_row(d)),
        ).start()
    for d in range(1, layers):
        send(
            pl_ref, pl_piece(layer, row), plz_send.at[d], pl_recv.at[layer, row], to(other_layer(d), row)
        ).start()
    for l in range(layers):

        @pl.when(layer == l)
        def _():
            for other in reversed(sources(l)):
                send(
                    own_strip(l), p_strip(l, row), pz_send.at[other], p_recv.at[l, row], to(other, row)
                ).start()
            for d in range(1, chips):
                send(
                    own_strip(l), p_strip(l, row), pf_send.at[l, d], p_recv.at[l, row],
                    to(layer, other_row(2 * d)),
                ).start()

    for l in range(layers):
        for s in range(count[l]):
            t = first[l] + s

            @pl.when(layer != l)
            def _():
                send(
                    tl_ref.at[t], zbuf.at[s, layer + 1], tl_send.at[t], tl_recv.at[s, layer], to(l, row)
                ).start()

    fbuf[...] = jnp.zeros_like(fbuf)
    eye = (
        lax.broadcasted_iota(jnp.int32, (rank, rank), 0) == lax.broadcasted_iota(jnp.int32, (rank, rank), 1)
    ).astype(F32)
    for copy in loads:
        copy.wait()
    for s in range(slots):
        t = own_first + jnp.minimum(s, own_count - 1)
        fbuf[s, 0:rank, 0:rank] = dot(orv[t, 0], skv[...], NT)
        fbuf[s, 0:rank, rank : 2 * rank] = eye

    for d in range(1, rows):
        here(pr_piece(other_row(d)), pr_recv.at[other_row(d)])
        here(pl_piece(layer, other_row(d)), pl_recv.at[layer, other_row(d)])
    coupling = dot(trv[...].reshape(tiles * rank, width), prw[...], NT)
    sketched = dot(plw[layer], skv[...], NT)
    chained = dot(coupling, sketched, NN, HIGHEST)
    for t in range(tiles):
        weight = -(mask_ref[t].astype(F32))
        block = slice(t * rank, (t + 1) * rank)
        ce[t, :, 0:rank] = chained[block] * weight
        ce[t, :, rank : 2 * rank] = coupling[block] * weight
    for l in range(layers):
        for s in range(count[l]):
            t = first[l] + s

            @pl.when(layer != l)
            def _():
                send(
                    ce.at[t], cebuf.at[s, layer], ce_send.at[t], ce_recv.at[s, layer], to(l, row)
                ).start()

            @pl.when(layer == l)
            def _():
                cebuf[s, layer] = ce[t]

    for me in range(layers):

        @pl.when(layer == me)
        def _():
            for l in sources(me):
                here(pl_piece(l, row), pl_recv.at[l, row])
                for d in range(1, rows):
                    send(
                        pl_piece(l, row), pl_piece(l, row), plf_send.at[l, d], pl_recv.at[l, row],
                        to(layer, other_row(d)),
                    ).start()
                here(p_strip(l, row), p_recv.at[l, row])
                for d in range(1, chips):
                    send(
                        p_strip(l, row), p_strip(l, row), pf_send.at[l, d], p_recv.at[l, row],
                        to(layer, other_row(2 * d)),
                    ).start()
            share_strips(me)

    for l in range(layers):

        @pl.when(layer == l)
        def _():
            for s in range(count[l]):
                for k in range(layers):
                    if k != l:
                        here(zbuf.at[s, k + 1], tl_recv.at[s, k])
                        here(cebuf.at[s, k], ce_recv.at[s, k])

    parts = []
    for s in range(slots):
        at = jnp.minimum(s, own_count - 1)
        z = zbuf[at].reshape((layers + 1) * rank, width)
        gram = dot(z, z, NT)
        for k in range(layers):
            block = slice((k + 1) * rank, (k + 2) * rank)
            fbuf[s, block, 0:rank] = cebuf[at, k, :, 0:rank]
            fbuf[s, block, (k + 2) * rank : (k + 3) * rank] = cebuf[at, k, :, rank : 2 * rank]
        joined = dot6(fbuf[s, :, 0:rank].T, gram)
        parts.append(dot6(joined, fbuf[s])[None])
    found = eliminate(jnp.concatenate(parts, axis=0), rank)
    for l in range(layers):

        @pl.when(layer == l)
        def _():
            for s in range(count[l]):
                t = first[l] + s
                high, low = split(found[s][:, rank:])
                mall[t, :, 0:rank] = high[:, 0:rank]
                mall[t, :, rank : 2 * rank] = low[:, 0:rank]
                mall[t, :, 2 * rank : (layers + 2) * rank] = high[:, rank:]
                mall[t, :, (layers + 2) * rank :] = low[:, rank:]
                for d in range(1, layers):
                    send(
                        mall.at[t], mall.at[t], m_send.at[t, d], m_recv.at[t], to(other_layer(d), row)
                    ).start()

    for me in range(layers):

        @pl.when(layer == me)
        def _():
            for l in sources(me):
                share_strips(l)

    for l in range(layers):
        for d in range(chips):
            r = lax.rem(sibling + 2 * d, rows)
            here(p_strip(l, r), p_recv.at[l, r])
    chunk = 256
    half = chunk // 2
    chunks = width // chunk
    inverses = invert_lower(
        [pw[i * half : (i + 1) * half, i * half : (i + 1) * half] for i in range(2 * chunks)], half
    )
    inner = [
        dot(pw[c * chunk + half : (c + 1) * chunk, c * chunk : c * chunk + half], inverses[2 * c], NN, HIGHEST)
        for c in range(chunks)
    ]
    for c in range(chunks):
        cross = dot(inverses[2 * c + 1], inner[c], NN, HIGHEST)
        for part, value in enumerate(split(inverses[2 * c])):
            diag[part, c, 0:half, 0:half] = value
        for part, value in enumerate(split(inverses[2 * c + 1])):
            diag[part, c, half:chunk, half:chunk] = value
        for part, value in enumerate(split(-cross)):
            diag[part, c, half:chunk, 0:half] = value
            diag[part, c, 0:half, half:chunk] = jnp.zeros_like(value)
        if c:
            rows_at = slice(c * chunk, (c + 1) * chunk)
            for part, value in enumerate(split(pw[rows_at, 0 : c * chunk])):
                below[part, rows_at, 0 : c * chunk] = value

    for l in range(layers):

        @pl.when(layer != l)
        def _():
            for d in range(1, rows):
                here(pl_piece(l, other_row(d)), pl_recv.at[l, other_row(d)])
            for s in range(count[l]):
                here(mall.at[first[l] + s], m_recv.at[first[l] + s])

    panels = plw[...].reshape(layers * rank, width)
    for t in range(tiles):
        core[t * rank : (t + 1) * rank, :] = dot(
            mall[t, :, 0 : 2 * rank], orv[t].reshape(2 * rank, width), NN
        )
    high = mall[:, :, 2 * rank : (layers + 2) * rank].reshape(tiles * rank, layers * rank)
    low = mall[:, :, (layers + 2) * rank :].reshape(tiles * rank, layers * rank)
    solved = []
    outs = []
    for c in range(chunks):
        cols = slice(c * chunk, (c + 1) * chunk)
        rest = core[:, cols] + (dot(high, panels[:, cols], NN) + dot(low, panels[:, cols], NN))
        for i in range(c):
            at = slice(i * chunk, (i + 1) * chunk)
            rest = rest - dot3(solved[i], (below[0, cols, at], below[1, cols, at]), NT)
        x = dot3(split(rest), (diag[0, c], diag[1, c]), NT)
        xv[:, :, cols] = x.reshape(tiles, rank, chunk)
        outs.append(
            pltpu.make_async_copy(
                xv.at[:, :, pl.ds(c * chunk, chunk)], out_ref.at[:, :, pl.ds(c * chunk, chunk)], leave.at[c]
            )
        )
        outs[-1].start()
        if c + 1 < chunks:
            solved.append(split(x))

    for copy in outs:
        copy.wait()
    for d in range(1, rows):
        sent(pr_piece(row), pr_send.at[d])
        sent(pl_piece(layer, row), pl_send.at[d])
    for d in range(1, layers):
        sent(pl_piece(layer, row), plz_send.at[d])
    for l in range(layers):
        for d in range(1, chips):
            sent(p_strip(l, row), pf_send.at[l, d])
        for d in range(chips):
            sent(p_strip(l, other_row(2 * d)), p3_send.at[l, d])

        @pl.when(layer == l)
        def _():
            for other in sources(l):
                sent(p_strip(l, row), pz_send.at[other])
            for d in range(1, layers):
                for s in range(count[l]):
                    sent(mall.at[first[l] + s], m_send.at[first[l] + s, d])

        @pl.when(layer != l)
        def _():
            for d in range(1, rows):
                sent(pl_piece(l, row), plf_send.at[l, d])
            for s in range(count[l]):
                sent(tl_ref.at[first[l] + s], tl_send.at[first[l] + s])
                sent(ce.at[first[l] + s], ce_send.at[first[l] + s])


def shards_kernel(layers, rows, tile_left, tile_right, tile_mask, orig_left, orig_right, pivot_left, pivot_right, sketch, pivot_factor):
    tiles, _, rank, width = tile_left.shape
    slots = max(owners(tiles, layers)[0])
    dma = pltpu.SemaphoreType.DMA
    hbm = pl.BlockSpec(memory_space=pltpu.HBM)
    lanes = (layers + 2) * rank
    return pl.pallas_call(
        partial(kernel, layers, rows),
        out_shape=jax.ShapeDtypeStruct((tiles, rank, width), F32),
        in_specs=[pl.BlockSpec(memory_space=pltpu.SMEM)] + [hbm] * 8,
        out_specs=hbm,
        scratch_shapes=[
            pltpu.VMEM((rank, width), BF16),
            pltpu.VMEM((layers, rank, width), BF16),
            pltpu.VMEM((width, width), F32),
            pltpu.VMEM((slots, layers + 1, rank, width), BF16),
            pltpu.VMEM((tiles, rank, 2 * rank), F32),
            pltpu.VMEM((slots, layers, rank, 2 * rank), F32),
            pltpu.VMEM((slots, (layers + 1) * rank, lanes), F32),
            pltpu.VMEM((tiles, rank, 2 * (layers + 1) * rank), BF16),
            pltpu.VMEM((2, width // 256, 256, 256), BF16),
            pltpu.VMEM((2, width, width), BF16),
            pltpu.VMEM((tiles * rank, width), F32),
            pltpu.VMEM((tiles, rank, width), BF16),
            pltpu.VMEM((tiles, 2, rank, width), BF16),
            pltpu.VMEM((rank, width), BF16),
            pltpu.VMEM((tiles, rank, width), F32),
            dma((rows,)), dma((rows,)), dma((rows,)), dma((layers, rows)),
            dma((layers,)), dma((layers, rows)), dma((layers, rows)), dma((layers, rows)),
            dma((layers,)), dma((layers, rows)),
            dma((tiles,)), dma((slots, layers)), dma((tiles,)), dma((slots, layers)),
            dma((tiles, layers)), dma((tiles,)), dma((7,)), dma((2, slots)), dma((width // 256,)),
        ],
        compiler_params=pltpu.CompilerParams(
            collective_id=0, has_side_effects=True, vmem_limit_bytes=63 * 1024 * 1024
        ),
    )(
        tile_mask.reshape(tiles), tile_left.reshape(tiles, rank, width), tile_right.reshape(tiles, rank, width),
        orig_left, orig_right, pivot_left.reshape(rank, -1), pivot_right.reshape(rank, -1),
        sketch, pivot_factor,
    )


def shards_general(
    tile_left,
    tile_right,
    tile_mask,
    orig_left,
    orig_right,
    pivot_left,
    pivot_right,
    sketch,
    pivot_factor,
):
    highest = HIGHEST
    pivot_whole = lax.all_gather(pivot_factor, ("layer", "row"), axis=0, tiled=True)
    left_whole, right_whole = (
        lax.all_gather(pivot_left, "row", axis=2, tiled=True),
        lax.all_gather(pivot_right, "row", axis=2, tiled=True),
    )
    coupling = jnp.einsum("tpqb,psb->tpqs", tile_right, right_whole, preferred_element_type=F32)
    weights = tile_mask.astype(F32)[:, :, None, None]
    update_left = jnp.einsum("tpqs,tpqb->tpsb", coupling, tile_left.astype(F32), precision=highest) * weights
    sketched = jnp.einsum("pqb,sb->pqs", left_whole, sketch, preferred_element_type=F32)
    partial_sample = jnp.einsum("tpqb,pqs->tsb", update_left, sketched, precision=highest)
    orig_float = orig_left.astype(F32)
    orig_sketch = jnp.einsum("tqb,sb->tqs", orig_right, sketch, preferred_element_type=F32)
    own_sample = jnp.einsum("tqb,tqs->tsb", orig_float, orig_sketch, precision=highest)
    sample = own_sample - lax.psum(partial_sample, "layer")
    gram_matrix = jnp.einsum("tqb,tsb->tqs", sample, sample, precision=highest)
    factor = jnp.linalg.cholesky(gram_matrix)
    row_basis = jax.vmap(partial(jax.scipy.linalg.solve_triangular, lower=True))(factor, sample)
    projected = jnp.einsum("tpqb,tsb->tpqs", update_left, row_basis, precision=highest)
    partial_core = jnp.einsum("pqb,tpqs->tsb", left_whole.astype(F32), projected, precision=highest)
    orig_basis = jnp.einsum("tqb,tsb->tqs", orig_float, row_basis, precision=highest)
    own_core = jnp.einsum("tqb,tqs->tsb", orig_right.astype(F32), orig_basis, precision=highest)
    core = own_core - lax.psum(partial_core, "layer")
    tile_count, rank_rows, cell_count = core.shape
    right_sides = core.reshape(tile_count * rank_rows, cell_count).T
    solution = jax.scipy.linalg.solve_triangular(pivot_whole, right_sides, lower=True)
    return solution.T.reshape(tile_count, rank_rows, cell_count)


def solution(mesh):
    in_specs = (
        P("row", "layer", None, None),
        P("row", "layer", None, None),
        P("row", "layer"),
        P("row", None, None),
        P("row", None, None),
        P("layer", None, "row"),
        P("layer", None, "row"),
        P(),
        P(("layer", "row"), None),
    )
    out_specs = P("row", None, None)
    layers, rows = mesh.shape["layer"], mesh.shape["row"]

    def shards(*blocks):
        tiles, panels, rank, width = blocks[0].shape
        fits = (
            panels == 1 and tiles >= layers and rank == 64 and width % 256 == 0 and rows % 2 == 0
            and width % (128 * rows) == 0 and width % (8 * layers * rows) == 0
        )
        if fits:
            return shards_kernel(layers, rows, *blocks)
        return shards_general(*blocks)

    return jax.shard_map(shards, mesh=mesh, in_specs=in_specs, out_specs=out_specs, check_vma=False)
```
